32 devices in a mesh: grp: 4 (over y, x), inner: 8 (over z, core).
Axes of the slice: x: 2, y: 2, z: 4, core: 2. Of those that a mesh axis runs over, the one named last changes fastest.
Arguments:
- embeds: bfloat16 [4096, 1024], P(('grp', 'inner')), may hold values from -1.05 to 1.05
- fine_centroids: bfloat16 [8192, 1024], P('inner'), may hold values from -1.05 to 1.05
- coarse_centroids: bfloat16 [512, 1024], replicated, may hold values from -0.39375 to 0.39375
Outputs:
- fine_update: float32 [8192, 1024], P('inner')
- coarse_update: float32 [512, 1024], replicated
The draws below stay inside these ranges and needn't reach their ends.
All inputs are finite; a program needn't handle non-finite values.
Results may differ from the reference program's by a relative error of at most 0.0044.
Values may be sent and summed in bfloat16 or wider, within the bound.
A program may use at most 64 MiB of HBM per device.

```python
import jax
import jax.numpy as jnp
from jax import lax

D = 1024
C = 512
K = 8192
ROWS = 4096


def centroid_tables(key):
    coarse_table = jax.random.truncated_normal(jax.random.fold_in(key, 12), -3.0, 3.0, (C, D), jnp.float32) * D ** (-0.5)
    fine_table = jax.random.truncated_normal(jax.random.fold_in(key, 11), -3.0, 3.0, (K, D), jnp.float32) * D ** (-0.5)
    return (fine_table, coarse_table)


def draw_fine_centroids(key, part):
    fine_table, coarse_table = centroid_tables(key)
    return fine_table.astype(jnp.bfloat16)


def draw_coarse_centroids(key, part):
    fine_table, coarse_table = centroid_tables(key)
    return coarse_table.astype(jnp.bfloat16)


def draw_embeds(key, part):
    values = jax.random.truncated_normal(jax.random.fold_in(key, 13), -3.0, 3.0, (ROWS, D), jnp.float32) * D ** (-0.5)
    return values.astype(jnp.bfloat16)


def setup_inputs(seed: int = 0) -> dict:
    arg_keys = jax.random.split(jax.random.key(seed), 4)
    return {
        "embeds": draw_embeds(jax.random.fold_in(arg_keys[3], 71), 0),
        "fine_centroids": draw_fine_centroids(jax.random.fold_in(arg_keys[3], 71), 0),
        "coarse_centroids": draw_coarse_centroids(jax.random.fold_in(arg_keys[3], 71), 0),
    }


temper = 0.02
shrink = 1.0
anchor = 8.0


def coarse_softmax(fine_low, coarse_cent, coarse_sq):
    logits = (lax.dot_general(fine_low, coarse_cent, (((1,), (1,)), ((), ())), preferred_element_type=jnp.float32) - 0.5 * coarse_sq) / temper
    shifted = jnp.exp(logits - jnp.max(logits, axis=1, keepdims=True))
    return shifted / jnp.sum(shifted, axis=1, keepdims=True)


def reference(embeds, fine_centroids, coarse_centroids):
    fine_sq = jnp.sum(jnp.square(fine_centroids.astype(jnp.float32)), axis=1)
    coarse_sq = jnp.sum(jnp.square(coarse_centroids.astype(jnp.float32)), axis=1)
    total_rows = embeds.shape[0]
    block_size = min(512, total_rows)
    blocks = embeds.reshape(total_rows // block_size, block_size, embeds.shape[1])

    def accumulate(running, row_block):
        scores = (lax.dot_general(row_block, fine_centroids, (((1,), (1,)), ((), ())), preferred_element_type=jnp.float32) - 0.5 * fine_sq) / temper
        shifted = jnp.exp(scores - jnp.max(scores, axis=1, keepdims=True))
        resp_low = (shifted / jnp.sum(shifted, axis=1, keepdims=True)).astype(jnp.bfloat16)
        moment = running[0] + lax.dot_general(resp_low, row_block, (((0,), (0,)), ((), ())), preferred_element_type=jnp.float32)
        mass_sum = running[1] + jnp.sum(resp_low, axis=0, dtype=jnp.float32)
        return (moment, mass_sum), None

    start_state = (jnp.zeros((fine_centroids.shape[0], embeds.shape[1]), jnp.float32), jnp.zeros((fine_centroids.shape[0],), jnp.float32))
    (moment, mass_sum), unused = lax.scan(accumulate, start_state, blocks)
    parent = coarse_softmax(fine_centroids, coarse_centroids, coarse_sq).astype(jnp.bfloat16)
    prior_mean = jnp.dot(parent, coarse_centroids, preferred_element_type=jnp.float32)
    weight = mass_sum + shrink
    fine_update = (moment + shrink * prior_mean) / weight[:, None]
    fine_low = fine_update.astype(jnp.bfloat16)
    child_prob = coarse_softmax(fine_low, coarse_centroids, coarse_sq)
    share_low = (child_prob * weight[:, None]).astype(jnp.bfloat16)
    numerator = lax.dot_general(share_low, fine_low, (((0,), (0,)), ((), ())), preferred_element_type=jnp.float32)
    denominator = jnp.sum(share_low, axis=0, dtype=jnp.float32)
    coarse_update = (numerator + anchor * coarse_centroids.astype(jnp.float32)) / (denominator[:, None] + anchor)
    return fine_update, coarse_update
```

```python
import functools

import jax
import jax.numpy as jnp
from jax import lax
from jax.experimental import pallas as pl
from jax.experimental.pallas import tpu as pltpu
from jax.sharding import PartitionSpec as P

temper = 0.02
shrink = 1.0
anchor = 8.0
MESH = pl.DeviceIdType.MESH
F32 = jnp.float32
BF16 = jnp.bfloat16
NT = (((1,), (1,)), ((), ()))
TN = (((0,), (0,)), ((), ()))


def tile_of(n, most=256):
    return most if n % most == 0 else n


def ring_place(g, groups):
    half = groups // 2
    return jnp.where(g < half, g, 3 * half - 1 - g)


def gather_kernel(
    groups, inner, with_prior,
    e_ref, fine_ref, coarse_ref,
    moment_ref, mass_ref,
    rows, prob, sbuf, half_sq, mass, peak, stat,
    up_send, down_send, z_recv, ring_send, ring_recv, sib_send, sib_recv, stat_send, stat_recv,
):
    layers = inner // 2
    reach = groups // 2
    count = e_ref.shape[0]
    both = 2 * count
    part = count // 2
    width = e_ref.shape[1]
    kl = fine_ref.shape[0]
    kt = tile_of(kl)
    g = lax.axis_index("grp")
    i = lax.axis_index("inner")
    z = i // 2
    core = i % 2
    place = ring_place(g, groups)
    ahead = ring_place((place + 1) % groups, groups)
    behind = ring_place((place + groups - 1) % groups, groups)
    sibling = (g, 2 * z + 1 - core)

    barrier = pltpu.get_barrier_semaphore()
    for off in range(1, inner):
        pl.semaphore_signal(barrier, inc=1, device_id=(g, (i + off) % inner), device_id_type=MESH)
    for other in (ahead, behind):
        pl.semaphore_signal(barrier, inc=1, device_id=(other, i), device_id_type=MESH)
    pl.semaphore_wait(barrier, inner + 1)

    low = jnp.minimum(z, layers - 1 - z)
    side = jnp.where(2 * z < layers - 1, 1, -1)

    def layer_at(q):
        near = z + ((q + 1) // 2) * (1 - 2 * (q % 2))
        return jnp.where(q <= 2 * low, near, z + side * (q - low))

    def slots_of(h):
        if h == 0:
            return (0,)
        if h == reach:
            return (groups - 1,)
        return (2 * h - 1, 2 * h)

    def up_copy(zz):
        block = rows.at[zz, 0, core]
        return pltpu.make_async_remote_copy(
            block, block, up_send.at[zz], z_recv.at[zz], (g, i + 2), device_id_type=MESH)

    def down_copy(zz):
        block = rows.at[zz, 0, core]
        return pltpu.make_async_remote_copy(
            block, block, down_send.at[zz], z_recv.at[zz], (g, i - 2), device_id_type=MESH)

    def ring_copy(zz, hop, way):
        source = 0 if hop == 1 else 2 * (hop - 1) - 1 + way
        if hop < reach:
            src, dst = rows.at[zz, source, core], rows.at[zz, 2 * hop - 1 + way, core]
        else:
            piece = pl.ds(way * part, part)
            src, dst = rows.at[zz, source, core, piece], rows.at[zz, groups - 1, core, piece]
        return pltpu.make_async_remote_copy(
            src, dst, ring_send.at[way, zz, hop - 1], ring_recv.at[way, zz, hop - 1],
            (ahead if way == 0 else behind, i), device_id_type=MESH)

    def sib_copy(zz, slot):
        block = rows.at[zz, slot, core]
        return pltpu.make_async_remote_copy(
            block, block, sib_send.at[zz, slot], sib_recv.at[zz, slot], sibling, device_id_type=MESH)

    def sib_arrival(zz, slot):
        block = rows.at[zz, slot, 1 - core]
        return pltpu.make_async_remote_copy(
            block, block, sib_send.at[zz, slot], sib_recv.at[zz, slot], sibling, device_id_type=MESH)

    def goes_up(zz):
        return jnp.logical_and(zz <= z, z < layers - 1)

    def goes_down(zz):
        return jnp.logical_and(zz >= z, z > 0)

    def forward(h, q):
        zz = layer_at(q)
        if h == 0:
            @pl.when(q > 0)
            def _():
                up_copy(zz).wait_recv()

            @pl.when(goes_up(zz))
            def _():
                up_copy(zz).start()

            @pl.when(goes_down(zz))
            def _():
                down_copy(zz).start()
        else:
            for way in (0, 1):
                ring_copy(zz, h, way).wait_recv()
        if h < reach:
            for way in (0, 1):
                ring_copy(zz, h + 1, way).start()
        for slot in slots_of(h):
            sib_copy(zz, slot).start()

    def stat_copy(zz, h, peer):
        slots = slots_of(h)
        piece = stat.at[zz, i, pl.ds(slots[0], len(slots))]
        return pltpu.make_async_remote_copy(
            piece, piece, stat_send.at[zz, h], stat_recv.at[zz, h], (g, peer), device_id_type=MESH)

    def stat_all(zz, h):
        slots = slots_of(h)
        piece = stat.at[zz, pl.ds(0, inner - 1), pl.ds(slots[0], len(slots))]
        return pltpu.make_async_remote_copy(
            piece, piece, stat_send.at[zz, h], stat_recv.at[zz, h], (g, (i + 1) % inner), device_id_type=MESH)

    def score(h, q):
        zz = layer_at(q)
        for slot in slots_of(h):
            sib_arrival(zz, slot).wait_recv()
            block = rows[zz, slot].reshape(both, width)

            def first(t, top):
                ks = pl.ds(pl.multiple_of(t * kt, kt), kt)
                s = lax.dot_general(fine_ref[ks, :], block, NT, preferred_element_type=F32)
                s = s * (1.0 / temper) - half_sq[ks, :]
                sbuf[ks, :] = s
                return jnp.maximum(top, jnp.max(s, axis=0, keepdims=True))

            top = lax.fori_loop(0, kl // kt, first, jnp.full((1, both), -jnp.inf, F32))

            def second(t, total):
                ks = pl.ds(pl.multiple_of(t * kt, kt), kt)
                e = jnp.exp(sbuf[ks, :] - top)
                prob[zz, slot, ks, :] = e.astype(BF16)
                return total + jnp.sum(e, axis=0, keepdims=True)

            total = lax.fori_loop(0, kl // kt, second, jnp.zeros((1, both), F32))
            peak[zz, slot] = top
            stat[zz, i, slot] = top + jnp.log(total)
        for off in range(1, inner):
            stat_copy(zz, h, (i + off) % inner).start()

    def moments(h, u):
        items = []
        for zz in (layers // 2 - 1 - u, layers // 2 + u):
            stat_all(zz, h).wait_recv()
            for slot in slots_of(h):
                lse = stat[zz, :, slot]
                most = jnp.max(lse, axis=0)
                lse = most + jnp.log(jnp.sum(jnp.exp(lse - most[None]), axis=0))
                items.append((zz, slot, jnp.exp(peak[zz, slot] - lse)))

        def step(t, carry):
            ks = pl.ds(pl.multiple_of(t * kt, kt), kt)
            acc = moment_ref[ks, :]
            seen = mass[ks, :]
            for zz, slot, scale in items:
                resp = prob[zz, slot, ks, :].astype(F32) * scale
                seen = seen + resp
                acc = acc + jnp.dot(
                    resp.astype(BF16), rows[zz, slot].reshape(both, width), preferred_element_type=F32)
            moment_ref[ks, :] = acc
            mass[ks, :] = seen
            return carry

        lax.fori_loop(0, kl // kt, step, 0)

    rows[z, 0, core] = e_ref[...]
    forward(0, 0)

    def squares(t, carry):
        ks = pl.ds(pl.multiple_of(t * kt, kt), kt)
        f = fine_ref[ks, :].astype(F32)
        half_sq[ks, :] = jnp.broadcast_to(
            (0.5 / temper) * jnp.sum(f * f, axis=1, keepdims=True), (kt, both))
        mass[ks, :] = jnp.zeros((kt, both), F32)
        if not with_prior:
            moment_ref[ks, :] = jnp.zeros((kt, width), F32)
        return carry

    lax.fori_loop(0, kl // kt, squares, 0)
    if with_prior:
        c = coarse_ref[...].astype(F32)
        c_sq = jnp.broadcast_to(jnp.sum(c * c, axis=1, keepdims=True), (c.shape[0], 128))
        c_half = (0.5 / temper) * jnp.transpose(c_sq)[0:1, :]

        def prior(t, carry):
            ks = pl.ds(pl.multiple_of(t * kt, kt), kt)
            logits = lax.dot_general(fine_ref[ks, :], coarse_ref[...], NT, preferred_element_type=F32)
            logits = logits * (1.0 / temper) - c_half
            e = jnp.exp(logits - jnp.max(logits, axis=1, keepdims=True))
            parent = (e / jnp.sum(e, axis=1, keepdims=True)).astype(BF16)
            moment_ref[ks, :] = shrink * jnp.dot(parent, coarse_ref[...], preferred_element_type=F32)
            return carry

        lax.fori_loop(0, kl // kt, prior, 0)

    def turn(t, carry):
        for h in range(reach + 1):
            q = t - h

            @pl.when(jnp.logical_and(jnp.logical_and(q >= 0, q < layers), t > 0))
            def _():
                forward(h, q)

        for h in range(reach + 1):
            q = t - h

            @pl.when(jnp.logical_and(q >= 0, q < layers))
            def _():
                score(h, q)

        for h in range(reach + 1):
            u = t - h - 1 - layers // 2

            @pl.when(jnp.logical_and(u >= 0, u < layers // 2))
            def _():
                moments(h, u)

        return carry

    lax.fori_loop(0, layers + reach + 1, turn, 0)

    mass_ref[...] = jnp.broadcast_to(jnp.sum(mass[...], axis=1, keepdims=True), mass_ref.shape)

    def drain(zz, carry):
        @pl.when(goes_up(zz))
        def _():
            up_copy(zz).wait_send()

        @pl.when(goes_down(zz))
        def _():
            down_copy(zz).wait_send()

        for h in range(reach + 1):
            if h < reach:
                for way in (0, 1):
                    ring_copy(zz, h + 1, way).wait_send()
            for slot in slots_of(h):
                sib_copy(zz, slot).wait_send()
            stat_all(zz, h).wait_send()
        return carry

    lax.fori_loop(0, layers, drain, 0)


def gathered_moments(groups, inner, number, embeds, fine, coarse):
    layers, reach = inner // 2, groups // 2
    count, width = embeds.shape
    kl = fine.shape[0]
    both = 2 * count
    dma = pltpu.SemaphoreType.DMA
    vm = pl.BlockSpec(memory_space=pltpu.VMEM)
    total = groups * inner * count
    return pl.pallas_call(
        functools.partial(gather_kernel, groups, inner, number == 0),
        out_shape=(
            jax.ShapeDtypeStruct((kl, width), F32),
            jax.ShapeDtypeStruct((kl, 128), F32),
        ),
        in_specs=[vm] * 3,
        out_specs=(vm, vm),
        scratch_shapes=[
            pltpu.VMEM((layers, groups, 2, count, width), BF16),
            pltpu.VMEM((layers, groups, kl, both), BF16),
            pltpu.VMEM((kl, both), F32),
            pltpu.VMEM((kl, both), F32),
            pltpu.VMEM((kl, both), F32),
            pltpu.VMEM((layers, groups, 1, both), F32),
            pltpu.VMEM((layers, inner, groups, 1, both), F32),
            dma((layers,)), dma((layers,)), dma((layers,)),
            dma((2, layers, reach)), dma((2, layers, reach)),
            dma((layers, groups)), dma((layers, groups)),
            dma((layers, reach + 1)), dma((layers, reach + 1)),
        ],
        compiler_params=pltpu.CompilerParams(
            collective_id=number, has_side_effects=True, vmem_limit_bytes=56 * 1024 * 1024),
        cost_estimate=pl.CostEstimate(
            flops=4 * total * kl * width, bytes_accessed=8 * kl * width, transcendentals=total * kl),
    )(embeds, fine, coarse)


def coarse_softmax(fine_low, coarse_cent, coarse_sq):
    logits = (lax.dot_general(fine_low, coarse_cent, NT, preferred_element_type=F32) - 0.5 * coarse_sq) / temper
    shifted = jnp.exp(logits - jnp.max(logits, axis=1, keepdims=True))
    return shifted / jnp.sum(shifted, axis=1, keepdims=True)


def on_device(groups, inner, embeds, fine_centroids, coarse_centroids):
    count, width = embeds.shape
    kl = fine_centroids.shape[0]
    rounds = 1
    while groups * inner * (count // rounds) * (width + kl) * 2 > 34 * 1024 * 1024:
        rounds *= 2
    step = count // rounds
    moment, mass = None, None
    for r in range(rounds):
        m, s = gathered_moments(
            groups, inner, r, embeds[r * step:(r + 1) * step], fine_centroids, coarse_centroids)
        moment = m if moment is None else moment + m
        mass = s if mass is None else mass + s
    weight = mass[:, :1] + shrink
    fine_update = moment / weight
    fine_low = fine_update.astype(BF16)
    coarse_sq = jnp.sum(jnp.square(coarse_centroids.astype(F32)), axis=1)
    share = (coarse_softmax(fine_low, coarse_centroids, coarse_sq) * weight).astype(BF16)
    numerator = lax.dot_general(share, fine_low, TN, preferred_element_type=F32)
    denominator = jnp.sum(share, axis=0, dtype=F32)
    numerator, denominator = lax.psum((numerator, denominator), "inner")
    coarse_update = (numerator + anchor * coarse_centroids.astype(F32)) / (denominator[:, None] + anchor)
    return (fine_update, coarse_update)


def solution(mesh):
    return jax.shard_map(
        functools.partial(on_device, mesh.shape["grp"], mesh.shape["inner"]),
        mesh=mesh,
        in_specs=(P(("grp", "inner"), None), P("inner", None), P()),
        out_specs=(P("inner", None), P()),
        check_vma=False,
    )
```

```python
import functools

import jax
import jax.numpy as jnp
from jax import lax
from jax.experimental import pallas as pl
from jax.experimental.pallas import tpu as pltpu
from jax.sharding import PartitionSpec as P

temper = 0.02
shrink = 1.0
anchor = 8.0
MESH = pl.DeviceIdType.MESH
F32 = jnp.float32
BF16 = jnp.bfloat16
NT = (((1,), (1,)), ((), ()))


def tile_of(n, most=256):
    return most if n % most == 0 else n


def ring_place(g, groups):
    half = groups // 2
    return jnp.where(g < half, g, 3 * half - 1 - g)


def gather_kernel(
    groups, inner, first_round, last_round, *refs,
):
    refs = list(refs)
    e_ref, fine_ref, coarse_ref = refs[:3]
    del refs[:3]
    if not first_round:
        moment_in, mass_in = refs[:2]
        del refs[:2]
    moment_ref, mass_ref = refs[:2]
    del refs[:2]
    if last_round:
        coarse_out = refs.pop(0)
    (rows, prob, half_sq, mass, peak, stat,
     up_send, down_send, z_recv, ring_send, ring_recv, sib_send, sib_recv, stat_send, stat_recv) = refs[:15]
    layers = inner // 2
    reach = groups // 2
    count = e_ref.shape[0]
    both = 2 * count
    part = count // 2
    width = e_ref.shape[1]
    kl = fine_ref.shape[0]
    kt = tile_of(kl)
    nt = tile_of(width)
    g = lax.axis_index("grp")
    i = lax.axis_index("inner")
    z = i // 2
    core = i % 2
    place = ring_place(g, groups)
    ahead = ring_place((place + 1) % groups, groups)
    behind = ring_place((place + groups - 1) % groups, groups)
    sibling = (g, 2 * z + 1 - core)

    barrier = pltpu.get_barrier_semaphore()
    for off in range(1, inner):
        pl.semaphore_signal(barrier, inc=1, device_id=(g, (i + off) % inner), device_id_type=MESH)
    for off in range(1, groups):
        pl.semaphore_signal(barrier, inc=1, device_id=((g + off) % groups, i), device_id_type=MESH)
    pl.semaphore_wait(barrier, inner + groups - 2)

    low = jnp.minimum(z, layers - 1 - z)
    side = jnp.where(2 * z < layers - 1, 1, -1)

    def layer_at(q):
        near = z + ((q + 1) // 2) * (1 - 2 * (q % 2))
        return jnp.where(q <= 2 * low, near, z + side * (q - low))

    def slots_of(h):
        if h == 0:
            return (0,)
        if h == reach:
            return (groups - 1,)
        return (2 * h - 1, 2 * h)

    def up_copy(zz):
        block = rows.at[zz, 0, core]
        return pltpu.make_async_remote_copy(
            block, block, up_send.at[zz], z_recv.at[zz], (g, i + 2), device_id_type=MESH)

    def down_copy(zz):
        block = rows.at[zz, 0, core]
        return pltpu.make_async_remote_copy(
            block, block, down_send.at[zz], z_recv.at[zz], (g, i - 2), device_id_type=MESH)

    def ring_copy(zz, hop, way):
        source = 0 if hop == 1 else 2 * (hop - 1) - 1 + way
        if hop < reach:
            src, dst = rows.at[zz, source, core], rows.at[zz, 2 * hop - 1 + way, core]
        else:
            piece = pl.ds(way * part, part)
            src, dst = rows.at[zz, source, core, piece], rows.at[zz, groups - 1, core, piece]
        return pltpu.make_async_remote_copy(
            src, dst, ring_send.at[way, zz, hop - 1], ring_recv.at[way, zz, hop - 1],
            (ahead if way == 0 else behind, i), device_id_type=MESH)

    def sib_copy(zz, slot):
        block = rows.at[zz, slot, core]
        return pltpu.make_async_remote_copy(
            block, block, sib_send.at[zz, slot], sib_recv.at[zz, slot], sibling, device_id_type=MESH)

    def sib_arrival(zz, slot):
        block = rows.at[zz, slot, 1 - core]
        return pltpu.make_async_remote_copy(
            block, block, sib_send.at[zz, slot], sib_recv.at[zz, slot], sibling, device_id_type=MESH)

    def goes_up(zz):
        return jnp.logical_and(zz <= z, z < layers - 1)

    def goes_down(zz):
        return jnp.logical_and(zz >= z, z > 0)

    def forward(h, q):
        zz = layer_at(q)
        if h == 0:
            @pl.when(q > 0)
            def _():
                up_copy(zz).wait_recv()

            @pl.when(goes_up(zz))
            def _():
                up_copy(zz).start()

            @pl.when(goes_down(zz))
            def _():
                down_copy(zz).start()
        else:
            for way in (0, 1):
                ring_copy(zz, h, way).wait_recv()
        if h < reach:
            for way in (0, 1):
                ring_copy(zz, h + 1, way).start()
        for slot in slots_of(h):
            sib_copy(zz, slot).start()

    def stat_copy(zz, h, peer):
        slots = slots_of(h)
        piece = stat.at[zz, i, pl.ds(slots[0], len(slots))]
        return pltpu.make_async_remote_copy(
            piece, piece, stat_send.at[zz, h], stat_recv.at[zz, h], (g, peer), device_id_type=MESH)

    def stat_all(zz, h):
        slots = slots_of(h)
        piece = stat.at[zz, pl.ds(0, inner - 1), pl.ds(slots[0], len(slots))]
        return pltpu.make_async_remote_copy(
            piece, piece, stat_send.at[zz, h], stat_recv.at[zz, h], (g, (i + 1) % inner), device_id_type=MESH)

    def score(h, q):
        zz = layer_at(q)
        for slot in slots_of(h):
            sib_arrival(zz, slot).wait_recv()
            block = rows[zz, slot].reshape(both, width)

            s = lax.dot_general(fine_ref[...], block, NT, preferred_element_type=F32)
            s = s * (1.0 / temper) - half_sq[...]
            top = jnp.max(s, axis=0, keepdims=True)
            e = jnp.exp(s - top)
            prob[zz, slot] = e.astype(BF16)
            total = jnp.sum(e, axis=0, keepdims=True)
            peak[zz, slot] = top
            stat[zz, i, slot] = top + jnp.log(total)
        for off in range(1, inner):
            stat_copy(zz, h, (i + off) % inner).start()

    def moments(h, u):
        items = []
        for zz in (layers // 2 - 1 - u, layers // 2 + u):
            stat_all(zz, h).wait_recv()
            for slot in slots_of(h):
                lse = stat[zz, :, slot]
                most = jnp.max(lse, axis=0)
                lse = most + jnp.log(jnp.sum(jnp.exp(lse - most[None]), axis=0))
                items.append((zz, slot, jnp.exp(peak[zz, slot] - lse)))

        def scaled(t, carry):
            ks = pl.ds(pl.multiple_of(t * kt, kt), kt)
            seen = mass[ks, :]
            for zz, slot, scale in items:
                resp = prob[zz, slot, ks, :].astype(F32) * scale
                seen = seen + resp
                prob[zz, slot, ks, :] = resp.astype(BF16)
            mass[ks, :] = seen
            return carry

        lax.fori_loop(0, kl // kt, scaled, 0)

        def step(t, carry):
            ds = pl.ds(pl.multiple_of(t * nt, nt), nt)
            acc = moment_ref[:, ds]
            for zz, slot, scale in items:
                acc = acc + jnp.dot(
                    prob[zz, slot], rows[zz, slot, :, :, ds].reshape(both, nt), preferred_element_type=F32)
            moment_ref[:, ds] = acc
            return carry

        lax.fori_loop(0, width // nt, step, 0)

    rows[z, 0, core] = e_ref[...]
    forward(0, 0)

    def squares(t, carry):
        ks = pl.ds(pl.multiple_of(t * kt, kt), kt)
        f = fine_ref[ks, :].astype(F32)
        half_sq[ks, :] = jnp.broadcast_to(
            (0.5 / temper) * jnp.sum(f * f, axis=1, keepdims=True), (kt, both))
        mass[ks, :] = jnp.zeros((kt, both), F32)
        if not first_round:
            moment_ref[ks, :] = moment_in[ks, :]
        return carry

    lax.fori_loop(0, kl // kt, squares, 0)
    if first_round:
        c = coarse_ref[...].astype(F32)
        c_sq = jnp.broadcast_to(jnp.sum(c * c, axis=1, keepdims=True), (c.shape[0], 128))
        c_half = (0.5 / temper) * jnp.transpose(c_sq)[0:1, :]

        def prior(t, carry):
            ks = pl.ds(pl.multiple_of(t * kt, kt), kt)
            logits = lax.dot_general(fine_ref[ks, :], coarse_ref[...], NT, preferred_element_type=F32)
            logits = logits * (1.0 / temper) - c_half
            e = jnp.exp(logits - jnp.max(logits, axis=1, keepdims=True))
            parent = (e / jnp.sum(e, axis=1, keepdims=True)).astype(BF16)
            moment_ref[ks, :] = shrink * jnp.dot(parent, coarse_ref[...], preferred_element_type=F32)
            return carry

        lax.fori_loop(0, kl // kt, prior, 0)

    def turn(t, carry):
        def gated(h, work):
            q = t - h

            @pl.when(jnp.logical_and(q >= 0, q < layers))
            def _():
                work(h, q)

        def forward_later(h, q):
            @pl.when(t > 0)
            def _():
                forward(h, q)

        for h in (0, 1):
            gated(h, forward_later)
        for h in (0, 1):
            gated(h, score)
        for h in range(reach + 1):
            u = t - h - 1 - layers // 2

            @pl.when(jnp.logical_and(u >= 0, u < layers // 2))
            def _():
                moments(h, u)

        for h in range(2, reach + 1):
            gated(h, forward)
            gated(h, score)
        return carry

    lax.fori_loop(0, layers + reach + 1, turn, 0)

    heavy = jnp.broadcast_to(jnp.sum(mass[...], axis=1, keepdims=True), mass_ref.shape)
    if not first_round:
        heavy = heavy + mass_in[...]
    mass_ref[...] = heavy
    if last_round:
        finish(groups, inner, coarse_ref, moment_ref, mass_ref, coarse_out, *refs[15:])

    def drain(zz, carry):
        @pl.when(goes_up(zz))
        def _():
            up_copy(zz).wait_send()

        @pl.when(goes_down(zz))
        def _():
            down_copy(zz).wait_send()

        for h in range(reach + 1):
            if h < reach:
                for way in (0, 1):
                    ring_copy(zz, h + 1, way).wait_send()
            for slot in slots_of(h):
                sib_copy(zz, slot).wait_send()
            stat_all(zz, h).wait_send()
        return carry

    lax.fori_loop(0, layers, drain, 0)


def shares_of(groups, inner, coarse_rows):
    piece = 16
    owners = min(inner // 2, coarse_rows // (groups * 2 * piece))
    return piece, owners


def finish(
    groups, inner, coarse_ref, moment_ref, mass_ref, coarse_out,
    fine_low, share, out1, in1, out2, in2, res,
    sem1, send2, recv2, send3, recv3, send4, recv4, send5, recv5,
):
    layers = inner // 2
    kl, width = moment_ref.shape
    coarse_rows = coarse_ref.shape[0]
    piece, owners = shares_of(groups, inner, coarse_rows)
    own_rows = 2 * owners * piece
    kt = tile_of(kl)
    g = lax.axis_index("grp")
    i = lax.axis_index("inner")
    z = i // 2
    core = i % 2
    sibling = (g, 2 * z + 1 - core)

    c = coarse_ref[...].astype(F32)
    c_half = (0.5 / temper) * jnp.sum(c * c, axis=1, keepdims=True)

    def child(t, carry):
        ks = pl.ds(pl.multiple_of(t * kt, kt), kt)
        weight = mass_ref[ks, :] + shrink
        new = moment_ref[ks, :] / weight[:, 0:1]
        moment_ref[ks, :] = new
        low = new.astype(BF16)
        fine_low[ks, :] = low
        logits = lax.dot_general(coarse_ref[...], low, NT, preferred_element_type=F32)
        logits = logits * (1.0 / temper) - c_half
        e = jnp.exp(logits - jnp.max(logits, axis=0, keepdims=True))
        scale = jnp.transpose(weight)[0:1, :] / jnp.sum(e, axis=0, keepdims=True)
        share[:, ks] = (e * scale).astype(BF16)
        return carry

    lax.fori_loop(0, kl // kt, child, 0)

    mine = share[pl.ds(pl.multiple_of(g * own_rows, own_rows), own_rows), :]
    numerator = jnp.dot(mine, fine_low[...], preferred_element_type=F32)
    den = jnp.broadcast_to(jnp.sum(mine.astype(F32), axis=1, keepdims=True), (own_rows, 128))

    def packed(total):
        high = total.astype(BF16)
        rest = (total - high.astype(F32)).astype(BF16)
        lane = lax.broadcasted_iota(jnp.int32, total.shape, total.ndim - 1)
        return jnp.where(lane < 64, high.astype(F32), rest.astype(F32)).astype(BF16)

    def unpacked(pair):
        return pair[..., 0:1] + pair[..., 64:65]

    shape = (2, owners, piece)
    out1[:, :, :, :width] = numerator.astype(BF16).reshape(*shape, width)
    out1[:, :, :, width:] = packed(den).reshape(*shape, 128)
    swap = pltpu.make_async_remote_copy(
        out1.at[1 - core], in1, sem1.at[0], sem1.at[1], sibling, device_id_type=MESH)
    swap.start()
    swap.wait_recv()
    a, b = out1[core].astype(F32), in1[...].astype(F32)
    out2[:, :, :width] = (a[..., :width] + b[..., :width]).astype(BF16)
    both_den = jnp.broadcast_to(unpacked(a[..., width:]) + unpacked(b[..., width:]), (owners, piece, 128))
    out2[:, :, width:] = packed(both_den)

    def part_copy(zo):
        return pltpu.make_async_remote_copy(
            out2.at[zo], in2.at[z], send2.at[zo], recv2.at[z], (g, 2 * zo + core), device_id_type=MESH)

    def part_arrival(zs):
        return pltpu.make_async_remote_copy(
            out2.at[0], in2.at[zs], send2.at[0], recv2.at[zs], (g, 2 * zs + core), device_id_type=MESH)

    def done_copy(zt):
        block = res.at[g, core, z]
        return pltpu.make_async_remote_copy(
            block, block, send3.at[zt], recv3.at[z], (g, 2 * zt + core), device_id_type=MESH)

    def done_arrival(zs):
        block = res.at[g, core, zs]
        return pltpu.make_async_remote_copy(
            block, block, send3.at[zs], recv3.at[zs], (g, 2 * zs + core), device_id_type=MESH)

    def when_owner(zo, work):
        if owners == layers:
            work()
        else:
            pl.when(zo < owners)(work)

    for off in range(1, layers):
        zo = (z + off) % layers
        when_owner(zo, lambda zo=zo: part_copy(zo).start())

    def own():
        for off in range(1, layers):
            part_arrival((z + off) % layers).wait_recv()
        in2[z] = out2[z]
        got = in2[...].astype(F32)
        num = jnp.sum(got[..., :width], axis=0)
        total = jnp.sum(unpacked(got[..., width:]), axis=0)
        at = pl.multiple_of(g * own_rows + (core * owners + z) * piece, piece)
        old = coarse_ref[pl.ds(at, piece), :].astype(F32)
        res[g, core, z] = ((num + anchor * old) / (total + anchor)).astype(BF16)
        for off in range(1, layers):
            done_copy((z + off) % layers).start()

    when_owner(z, own)
    for off in range(1, layers):
        zo = (z + off) % layers
        when_owner(zo, lambda zo=zo: done_arrival(zo).wait_recv())

    def group_copy(gt):
        block = res.at[g, core]
        return pltpu.make_async_remote_copy(
            block, block, send4.at[gt], recv4.at[g], (gt, i), device_id_type=MESH)

    def group_arrival(gs):
        block = res.at[gs, core]
        return pltpu.make_async_remote_copy(
            block, block, send4.at[gs], recv4.at[gs], (gs, i), device_id_type=MESH)

    def over(gs):
        block = res.at[gs, core]
        return pltpu.make_async_remote_copy(
            block, block, send5.at[gs], recv5.at[gs], sibling, device_id_type=MESH)

    def over_arrival(gs):
        block = res.at[gs, 1 - core]
        return pltpu.make_async_remote_copy(
            block, block, send5.at[gs], recv5.at[gs], sibling, device_id_type=MESH)

    for off in range(1, groups):
        group_copy((g + off) % groups).start()
    over(g).start()
    for off in range(1, groups):
        gs = (g + off) % groups
        group_arrival(gs).wait_recv()
        over(gs).start()
    for gs in range(groups):
        over_arrival(gs).wait_recv()
    coarse_out[...] = res[...].reshape(coarse_rows, width)

    swap.wait_send()
    for off in range(1, layers):
        zo = (z + off) % layers
        when_owner(zo, lambda zo=zo: part_copy(zo).wait_send())
        when_owner(z, lambda zo=zo: done_copy(zo).wait_send())
    for off in range(1, groups):
        group_copy((g + off) % groups).wait_send()
    for gs in range(groups):
        over(gs).wait_send()


def gathered_moments(groups, inner, number, rounds, embeds, fine, coarse, before):
    layers, reach = inner // 2, groups // 2
    count, width = embeds.shape
    kl = fine.shape[0]
    coarse_rows = coarse.shape[0]
    both = 2 * count
    dma = pltpu.SemaphoreType.DMA
    vm = pl.BlockSpec(memory_space=pltpu.VMEM)
    total = groups * inner * count
    last = number == rounds - 1
    out_shape = [jax.ShapeDtypeStruct((kl, width), F32), jax.ShapeDtypeStruct((kl, 128), F32)]
    scratch = [
        pltpu.VMEM((layers, groups, 2, count, width), BF16),
        pltpu.VMEM((layers, groups, kl, both), BF16),
        pltpu.VMEM((kl, both), F32),
        pltpu.VMEM((kl, both), F32),
        pltpu.VMEM((layers, groups, 1, both), F32),
        pltpu.VMEM((layers, inner, groups, 1, both), F32),
        dma((layers,)), dma((layers,)), dma((layers,)),
        dma((2, layers, reach)), dma((2, layers, reach)),
        dma((layers, groups)), dma((layers, groups)),
        dma((layers, reach + 1)), dma((layers, reach + 1)),
    ]
    if last:
        piece, owners = shares_of(groups, inner, coarse_rows)
        wide = width + 128
        out_shape.append(jax.ShapeDtypeStruct((coarse_rows, width), BF16))
        scratch += [
            pltpu.VMEM((kl, width), BF16),
            pltpu.VMEM((coarse_rows, kl), BF16),
            pltpu.VMEM((2, owners, piece, wide), BF16),
            pltpu.VMEM((owners, piece, wide), BF16),
            pltpu.VMEM((owners, piece, wide), BF16),
            pltpu.VMEM((layers, piece, wide), BF16),
            pltpu.VMEM((groups, 2, owners, piece, width), BF16),
            dma((2,)), dma((layers,)), dma((layers,)), dma((layers,)), dma((layers,)),
            dma((groups,)), dma((groups,)), dma((groups,)), dma((groups,)),
        ]
    args = (embeds, fine, coarse, *before)
    return pl.pallas_call(
        functools.partial(gather_kernel, groups, inner, number == 0, last),
        out_shape=out_shape,
        in_specs=[vm] * len(args),
        out_specs=[vm] * len(out_shape),
        scratch_shapes=scratch,
        compiler_params=pltpu.CompilerParams(
            collective_id=number, has_side_effects=True, vmem_limit_bytes=60 * 1024 * 1024),
        cost_estimate=pl.CostEstimate(
            flops=4 * total * kl * width, bytes_accessed=8 * kl * width, transcendentals=total * kl),
    )(*args)


def on_device(groups, inner, embeds, fine_centroids, coarse_centroids):
    count, width = embeds.shape
    kl = fine_centroids.shape[0]
    rounds = 1
    while groups * inner * (count // rounds) * (width + kl) * 2 > 34 * 1024 * 1024:
        rounds *= 2
    step = count // rounds
    found = ()
    for r in range(rounds):
        found = gathered_moments(
            groups, inner, r, rounds, embeds[r * step:(r + 1) * step], fine_centroids, coarse_centroids, found[:2])
    fine_update, _, coarse_update = found
    return (fine_update, coarse_update.astype(F32))


def solution(mesh):
    return jax.shard_map(
        functools.partial(on_device, mesh.shape["grp"], mesh.shape["inner"]),
        mesh=mesh,
        in_specs=(P(("grp", "inner"), None), P("inner", None), P()),
        out_specs=(P("inner", None), P()),
        check_vma=False,
    )
```

```python
import functools

import jax
import jax.numpy as jnp
from jax import lax
from jax.experimental import pallas as pl
from jax.experimental.pallas import tpu as pltpu
from jax.sharding import PartitionSpec as P

temper = 0.02
shrink = 1.0
anchor = 8.0
MESH = pl.DeviceIdType.MESH
F32 = jnp.float32
BF16 = jnp.bfloat16
NT = (((1,), (1,)), ((), ()))


def tile_of(n, most=256):
    return most if n % most == 0 else n


def ring_place(g, groups):
    half = groups // 2
    return jnp.where(g < half, g, 3 * half - 1 - g)


def gather_kernel(
    groups, inner, first_round, last_round, *refs,
):
    refs = list(refs)
    e_ref, fine_ref, coarse_ref = refs[:3]
    del refs[:3]
    if not first_round:
        moment_in, mass_in = refs[:2]
        del refs[:2]
    moment_ref, mass_ref = refs[:2]
    del refs[:2]
    if last_round:
        coarse_out = refs.pop(0)
    (rows, prob, moment, half_sq, mass, peak, stat,
     up_send, down_send, z_recv, ring_send, ring_recv, sib_send, sib_recv, stat_send, stat_recv, out_sem) = refs[:17]
    layers = inner // 2
    reach = groups // 2
    count = e_ref.shape[0]
    both = 2 * count
    part = count // 2
    width = e_ref.shape[1]
    kl = fine_ref.shape[0]
    kt = tile_of(kl)
    nt = tile_of(width)
    st = tile_of(kl, 512)
    g = lax.axis_index("grp")
    i = lax.axis_index("inner")
    z = i // 2
    core = i % 2
    place = ring_place(g, groups)
    ahead = ring_place((place + 1) % groups, groups)
    behind = ring_place((place + groups - 1) % groups, groups)
    sibling = (g, 2 * z + 1 - core)

    barrier = pltpu.get_barrier_semaphore()
    for off in range(1, inner):
        pl.semaphore_signal(barrier, inc=1, device_id=(g, (i + off) % inner), device_id_type=MESH)
    for off in range(1, groups):
        pl.semaphore_signal(barrier, inc=1, device_id=((g + off) % groups, i), device_id_type=MESH)
    pl.semaphore_wait(barrier, inner + groups - 2)

    low = jnp.minimum(z, layers - 1 - z)
    side = jnp.where(2 * z < layers - 1, 1, -1)

    def layer_at(q):
        near = z + ((q + 1) // 2) * (1 - 2 * (q % 2))
        return jnp.where(q <= 2 * low, near, z + side * (q - low))

    def slots_of(h):
        if h == 0:
            return (0,)
        if h == reach:
            return (groups - 1,)
        return (2 * h - 1, 2 * h)

    def up_copy(zz):
        block = rows.at[zz, 0, core]
        return pltpu.make_async_remote_copy(
            block, block, up_send.at[zz], z_recv.at[zz], (g, i + 2), device_id_type=MESH)

    def down_copy(zz):
        block = rows.at[zz, 0, core]
        return pltpu.make_async_remote_copy(
            block, block, down_send.at[zz], z_recv.at[zz], (g, i - 2), device_id_type=MESH)

    def ring_copy(zz, hop, way):
        source = 0 if hop == 1 else 2 * (hop - 1) - 1 + way
        if hop < reach:
            src, dst = rows.at[zz, source, core], rows.at[zz, 2 * hop - 1 + way, core]
        else:
            piece = pl.ds(way * part, part)
            src, dst = rows.at[zz, source, core, piece], rows.at[zz, groups - 1, core, piece]
        return pltpu.make_async_remote_copy(
            src, dst, ring_send.at[way, zz, hop - 1], ring_recv.at[way, zz, hop - 1],
            (ahead if way == 0 else behind, i), device_id_type=MESH)

    def sib_copy(zz, slot):
        block = rows.at[zz, slot, core]
        return pltpu.make_async_remote_copy(
            block, block, sib_send.at[zz, slot], sib_recv.at[zz, slot], sibling, device_id_type=MESH)

    def sib_arrival(zz, slot):
        block = rows.at[zz, slot, 1 - core]
        return pltpu.make_async_remote_copy(
            block, block, sib_send.at[zz, slot], sib_recv.at[zz, slot], sibling, device_id_type=MESH)

    def goes_up(zz):
        return jnp.logical_and(zz <= z, z < layers - 1)

    def goes_down(zz):
        return jnp.logical_and(zz >= z, z > 0)

    def forward(h, q):
        zz = layer_at(q)
        if h == 0:
            @pl.when(q > 0)
            def _():
                up_copy(zz).wait_recv()

            @pl.when(goes_up(zz))
            def _():
                up_copy(zz).start()

            @pl.when(goes_down(zz))
            def _():
                down_copy(zz).start()
        else:
            for way in (0, 1):
                ring_copy(zz, h, way).wait_recv()
        if h < reach:
            for way in (0, 1):
                ring_copy(zz, h + 1, way).start()
        for slot in slots_of(h):
            sib_copy(zz, slot).start()

    def stat_copy(zz, h, peer):
        slots = slots_of(h)
        piece = stat.at[zz, i, pl.ds(slots[0], len(slots))]
        return pltpu.make_async_remote_copy(
            piece, piece, stat_send.at[zz, h], stat_recv.at[zz, h], (g, peer), device_id_type=MESH)

    def stat_all(zz, h):
        slots = slots_of(h)
        piece = stat.at[zz, pl.ds(0, inner - 1), pl.ds(slots[0], len(slots))]
        return pltpu.make_async_remote_copy(
            piece, piece, stat_send.at[zz, h], stat_recv.at[zz, h], (g, (i + 1) % inner), device_id_type=MESH)

    def score(h, q):
        zz = layer_at(q)
        for slot in slots_of(h):
            sib_arrival(zz, slot).wait_recv()
        for slot in slots_of(h):
            block = rows[zz, slot].reshape(both, width)
            tops, totals = [], []
            for t in range(kl // st):
                ks = pl.ds(t * st, st)
                s = lax.dot_general(fine_ref[ks, :], block, NT, preferred_element_type=F32)
                s = s * (1.0 / temper) - half_sq[ks, :]
                top = jnp.max(s, axis=0, keepdims=True)
                e = jnp.exp(s - top)
                prob[zz, slot, ks, :] = e.astype(BF16)
                peak[zz, slot, t] = top
                tops.append(top)
                totals.append(jnp.sum(e, axis=0, keepdims=True))
            most = functools.reduce(jnp.maximum, tops)
            total = sum(a * jnp.exp(top - most) for a, top in zip(totals, tops))
            stat[zz, i, slot] = most + jnp.log(total)
        for off in range(1, inner):
            stat_copy(zz, h, (i + off) % inner).start()

    def moments(h, u):
        items = []
        for zz in (layers // 2 - 1 - u, layers // 2 + u):
            stat_all(zz, h).wait_recv()
            for slot in slots_of(h):
                lse = stat[zz, :, slot]
                most = jnp.max(lse, axis=0)
                lse = most + jnp.log(jnp.sum(jnp.exp(lse - most[None]), axis=0))
                items.append((zz, slot, lse))

        for t in range(kl // st):
            ks = pl.ds(t * st, st)
            seen = mass[ks, :]
            parts = []
            for zz, slot, lse in items:
                resp = prob[zz, slot, ks, :].astype(F32) * jnp.exp(peak[zz, slot, t] - lse)
                seen = seen + resp
                parts.append(resp.astype(BF16))
            mass[ks, :] = seen
            left = jnp.concatenate(parts, axis=1)
            for d in range(0, width, nt):
                ds = pl.ds(d, nt)
                right = jnp.concatenate(
                    [rows[zz, slot, :, :, ds].reshape(both, nt) for zz, slot, _ in items], axis=0)
                moment[ks, ds] += jnp.dot(left, right, preferred_element_type=F32)

    rows[z, 0, core] = e_ref[...]
    forward(0, 0)

    def squares(t, carry):
        ks = pl.ds(pl.multiple_of(t * kt, kt), kt)
        f = fine_ref[ks, :].astype(F32)
        half_sq[ks, :] = jnp.broadcast_to(
            (0.5 / temper) * jnp.sum(f * f, axis=1, keepdims=True), (kt, both))
        mass[ks, :] = jnp.zeros((kt, both), F32)
        if not first_round:
            moment[ks, :] = moment_in[ks, :]
        return carry

    lax.fori_loop(0, kl // kt, squares, 0)
    if first_round:
        c = coarse_ref[...].astype(F32)
        c_sq = jnp.broadcast_to(jnp.sum(c * c, axis=1, keepdims=True), (c.shape[0], 128))
        c_half = (0.5 / temper) * jnp.transpose(c_sq)[0:1, :]

        def prior(t, carry):
            ks = pl.ds(pl.multiple_of(t * kt, kt), kt)
            logits = lax.dot_general(fine_ref[ks, :], coarse_ref[...], NT, preferred_element_type=F32)
            logits = logits * (1.0 / temper) - c_half
            e = jnp.exp(logits - jnp.max(logits, axis=1, keepdims=True))
            parent = (e / jnp.sum(e, axis=1, keepdims=True)).astype(BF16)
            moment[ks, :] = shrink * jnp.dot(parent, coarse_ref[...], preferred_element_type=F32)
            return carry

        lax.fori_loop(0, kl // kt, prior, 0)

    def turn(t, carry):
        def gated(h, work):
            q = t - h

            @pl.when(jnp.logical_and(q >= 0, q < layers))
            def _():
                work(h, q)

        def forward_later(h, q):
            @pl.when(t > 0)
            def _():
                forward(h, q)

        for h in (0, 1):
            gated(h, forward_later)
        for h in (0, 1):
            gated(h, score)
        for h in range(reach + 1):
            u = t - h - 1 - layers // 2

            @pl.when(jnp.logical_and(u >= 0, u < layers // 2))
            def _():
                moments(h, u)

        for h in range(2, reach + 1):
            gated(h, forward)
            gated(h, score)
        return carry

    lax.fori_loop(0, layers + reach + 1, turn, 0)

    heavy = jnp.broadcast_to(jnp.sum(mass[...], axis=1, keepdims=True), mass_ref.shape)
    if not first_round:
        heavy = heavy + mass_in[...]
    mass_ref[...] = heavy
    written = pltpu.make_async_copy(moment, moment_ref, out_sem.at[0])
    written.start()
    if last_round:
        finish(groups, inner, coarse_ref, moment, mass_ref, coarse_out, *refs[17:])

    def drain(zz, carry):
        @pl.when(goes_up(zz))
        def _():
            up_copy(zz).wait_send()

        @pl.when(goes_down(zz))
        def _():
            down_copy(zz).wait_send()

        for h in range(reach + 1):
            if h < reach:
                for way in (0, 1):
                    ring_copy(zz, h + 1, way).wait_send()
            for slot in slots_of(h):
                sib_copy(zz, slot).wait_send()
            stat_all(zz, h).wait_send()
        return carry

    lax.fori_loop(0, layers, drain, 0)
    written.wait()


def shares_of(groups, inner, coarse_rows):
    piece = 16
    owners = min(inner // 2, coarse_rows // (groups * 2 * piece))
    return piece, owners


def finish(
    groups, inner, coarse_ref, moment_ref, mass_ref, coarse_out,
    fine_low, share, out1, in1, out2, in2, res,
    sem1, send2, recv2, send3, recv3, send4, recv4, send5, recv5,
):
    layers = inner // 2
    kl, width = moment_ref.shape
    coarse_rows = coarse_ref.shape[0]
    piece, owners = shares_of(groups, inner, coarse_rows)
    own_rows = 2 * owners * piece
    kt = tile_of(kl)
    g = lax.axis_index("grp")
    i = lax.axis_index("inner")
    z = i // 2
    core = i % 2
    sibling = (g, 2 * z + 1 - core)

    c = coarse_ref[...].astype(F32)
    c_half = (0.5 / temper) * jnp.sum(c * c, axis=1, keepdims=True)

    def child(t, carry):
        ks = pl.ds(pl.multiple_of(t * kt, kt), kt)
        weight = mass_ref[ks, :] + shrink
        low = (moment_ref[ks, :] * (1.0 / weight[:, 0:1])).astype(BF16)
        fine_low[ks, :] = low
        logits = lax.dot_general(coarse_ref[...], low, NT, preferred_element_type=F32)
        logits = logits * (1.0 / temper) - c_half
        e = jnp.exp(logits - jnp.max(logits, axis=0, keepdims=True))
        scale = jnp.transpose(weight)[0:1, :] / jnp.sum(e, axis=0, keepdims=True)
        share[:, ks] = (e * scale).astype(BF16)
        return carry

    lax.fori_loop(0, kl // kt, child, 0)

    mine = share[pl.ds(pl.multiple_of(g * own_rows, own_rows), own_rows), :]
    numerator = jnp.dot(mine, fine_low[...], preferred_element_type=F32)
    den = jnp.broadcast_to(jnp.sum(mine.astype(F32), axis=1, keepdims=True), (own_rows, 128))

    def packed(total):
        high = total.astype(BF16)
        rest = (total - high.astype(F32)).astype(BF16)
        lane = lax.broadcasted_iota(jnp.int32, total.shape, total.ndim - 1)
        return jnp.where(lane < 64, high.astype(F32), rest.astype(F32)).astype(BF16)

    def unpacked(pair):
        return pair[..., 0:1] + pair[..., 64:65]

    shape = (2, owners, piece)
    out1[:, :, :, :width] = numerator.astype(BF16).reshape(*shape, width)
    out1[:, :, :, width:] = packed(den).reshape(*shape, 128)
    swap = pltpu.make_async_remote_copy(
        out1.at[1 - core], in1, sem1.at[0], sem1.at[1], sibling, device_id_type=MESH)
    swap.start()
    swap.wait_recv()
    a, b = out1[core].astype(F32), in1[...].astype(F32)
    out2[:, :, :width] = (a[..., :width] + b[..., :width]).astype(BF16)
    both_den = jnp.broadcast_to(unpacked(a[..., width:]) + unpacked(b[..., width:]), (owners, piece, 128))
    out2[:, :, width:] = packed(both_den)

    def part_copy(zo):
        return pltpu.make_async_remote_copy(
            out2.at[zo], in2.at[z], send2.at[zo], recv2.at[z], (g, 2 * zo + core), device_id_type=MESH)

    def part_arrival(zs):
        return pltpu.make_async_remote_copy(
            out2.at[0], in2.at[zs], send2.at[0], recv2.at[zs], (g, 2 * zs + core), device_id_type=MESH)

    def done_copy(zt):
        block = res.at[g, core, z]
        return pltpu.make_async_remote_copy(
            block, block, send3.at[zt], recv3.at[z], (g, 2 * zt + core), device_id_type=MESH)

    def done_arrival(zs):
        block = res.at[g, core, zs]
        return pltpu.make_async_remote_copy(
            block, block, send3.at[zs], recv3.at[zs], (g, 2 * zs + core), device_id_type=MESH)

    def when_owner(zo, work):
        if owners == layers:
            work()
        else:
            pl.when(zo < owners)(work)

    for off in range(1, layers):
        zo = (z + off) % layers
        when_owner(zo, lambda zo=zo: part_copy(zo).start())

    def own():
        for off in range(1, layers):
            part_arrival((z + off) % layers).wait_recv()
        in2[z] = out2[z]
        got = in2[...].astype(F32)
        num = jnp.sum(got[..., :width], axis=0)
        total = jnp.sum(unpacked(got[..., width:]), axis=0)
        at = pl.multiple_of(g * own_rows + (core * owners + z) * piece, piece)
        old = coarse_ref[pl.ds(at, piece), :].astype(F32)
        res[g, core, z] = ((num + anchor * old) / (total + anchor)).astype(BF16)
        for off in range(1, layers):
            done_copy((z + off) % layers).start()

    when_owner(z, own)
    for off in range(1, layers):
        zo = (z + off) % layers
        when_owner(zo, lambda zo=zo: done_arrival(zo).wait_recv())

    def group_copy(gt):
        block = res.at[g, core]
        return pltpu.make_async_remote_copy(
            block, block, send4.at[gt], recv4.at[g], (gt, i), device_id_type=MESH)

    def group_arrival(gs):
        block = res.at[gs, core]
        return pltpu.make_async_remote_copy(
            block, block, send4.at[gs], recv4.at[gs], (gs, i), device_id_type=MESH)

    def over(gs):
        block = res.at[gs, core]
        return pltpu.make_async_remote_copy(
            block, block, send5.at[gs], recv5.at[gs], sibling, device_id_type=MESH)

    def over_arrival(gs):
        block = res.at[gs, 1 - core]
        return pltpu.make_async_remote_copy(
            block, block, send5.at[gs], recv5.at[gs], sibling, device_id_type=MESH)

    for off in range(1, groups):
        group_copy((g + off) % groups).start()
    over(g).start()
    for off in range(1, groups):
        gs = (g + off) % groups
        group_arrival(gs).wait_recv()
        over(gs).start()
    for gs in range(groups):
        over_arrival(gs).wait_recv()
    coarse_out[...] = res[...].reshape(coarse_rows, width)

    swap.wait_send()
    for off in range(1, layers):
        zo = (z + off) % layers
        when_owner(zo, lambda zo=zo: part_copy(zo).wait_send())
        when_owner(z, lambda zo=zo: done_copy(zo).wait_send())
    for off in range(1, groups):
        group_copy((g + off) % groups).wait_send()
    for gs in range(groups):
        over(gs).wait_send()


def gathered_moments(groups, inner, number, rounds, embeds, fine, coarse, before):
    layers, reach = inner // 2, groups // 2
    count, width = embeds.shape
    kl = fine.shape[0]
    coarse_rows = coarse.shape[0]
    both = 2 * count
    dma = pltpu.SemaphoreType.DMA
    vm = pl.BlockSpec(memory_space=pltpu.VMEM)
    total = groups * inner * count
    last = number == rounds - 1
    out_shape = [jax.ShapeDtypeStruct((kl, width), F32), jax.ShapeDtypeStruct((kl, 128), F32)]
    scratch = [
        pltpu.VMEM((layers, groups, 2, count, width), BF16),
        pltpu.VMEM((layers, groups, kl, both), BF16),
        pltpu.VMEM((kl, width), F32),
        pltpu.VMEM((kl, both), F32),
        pltpu.VMEM((kl, both), F32),
        pltpu.VMEM((layers, groups, kl // tile_of(kl, 512), 1, both), F32),
        pltpu.VMEM((layers, inner, groups, 1, both), F32),
        dma((layers,)), dma((layers,)), dma((layers,)),
        dma((2, layers, reach)), dma((2, layers, reach)),
        dma((layers, groups)), dma((layers, groups)),
        dma((layers, reach + 1)), dma((layers, reach + 1)), dma((1,)),
    ]
    if last:
        piece, owners = shares_of(groups, inner, coarse_rows)
        wide = width + 128
        out_shape.append(jax.ShapeDtypeStruct((coarse_rows, width), BF16))
        scratch += [
            pltpu.VMEM((kl, width), BF16),
            pltpu.VMEM((coarse_rows, kl), BF16),
            pltpu.VMEM((2, owners, piece, wide), BF16),
            pltpu.VMEM((owners, piece, wide), BF16),
            pltpu.VMEM((owners, piece, wide), BF16),
            pltpu.VMEM((layers, piece, wide), BF16),
            pltpu.VMEM((groups, 2, owners, piece, width), BF16),
            dma((2,)), dma((layers,)), dma((layers,)), dma((layers,)), dma((layers,)),
            dma((groups,)), dma((groups,)), dma((groups,)), dma((groups,)),
        ]
    args = (embeds, fine, coarse, *before)
    return pl.pallas_call(
        functools.partial(gather_kernel, groups, inner, number == 0, last),
        out_shape=out_shape,
        in_specs=[vm] * len(args),
        out_specs=[pl.BlockSpec(memory_space=pl.ANY)] + [vm] * (len(out_shape) - 1),
        scratch_shapes=scratch,
        compiler_params=pltpu.CompilerParams(
            collective_id=number, has_side_effects=True, vmem_limit_bytes=60 * 1024 * 1024),
        cost_estimate=pl.CostEstimate(
            flops=4 * total * kl * width, bytes_accessed=8 * kl * width, transcendentals=total * kl),
    )(*args)


def output_kernel(moment_ref, mass_ref, coarse_ref, fine_out, coarse_out):
    fine_out[...] = moment_ref[...] * (1.0 / (mass_ref[:, 0:1] + shrink))
    coarse_out[...] = coarse_ref[...].astype(F32)


def outputs(moment, mass, coarse):
    steps = 4
    kl, width = moment.shape
    coarse_rows = coarse.shape[0]

    def block(count, columns):
        return pl.BlockSpec((count // steps, columns), lambda t: (t, 0))

    return pl.pallas_call(
        output_kernel,
        grid=(steps,),
        out_shape=[jax.ShapeDtypeStruct((kl, width), F32), jax.ShapeDtypeStruct((coarse_rows, width), F32)],
        in_specs=[block(kl, width), block(kl, mass.shape[1]), block(coarse_rows, width)],
        out_specs=[block(kl, width), block(coarse_rows, width)],
    )(moment, mass, coarse)


def on_device(groups, inner, embeds, fine_centroids, coarse_centroids):
    count, width = embeds.shape
    kl = fine_centroids.shape[0]
    rounds = 1
    while groups * inner * (count // rounds) * (width + kl) * 2 > 34 * 1024 * 1024:
        rounds *= 2
    step = count // rounds
    found = ()
    for r in range(rounds):
        found = gathered_moments(
            groups, inner, r, rounds, embeds[r * step:(r + 1) * step], fine_centroids, coarse_centroids, found[:2])
    return tuple(outputs(*found))


def solution(mesh):
    return jax.shard_map(
        functools.partial(on_device, mesh.shape["grp"], mesh.shape["inner"]),
        mesh=mesh,
        in_specs=(P(("grp", "inner"), None), P("inner", None), P()),
        out_specs=(P("inner", None), P()),
        check_vma=False,
    )
```

```python
import functools

import jax
import jax.numpy as jnp
from jax import lax
from jax.experimental import pallas as pl
from jax.experimental.pallas import tpu as pltpu
from jax.sharding import PartitionSpec as P

temper = 0.02
shrink = 1.0
anchor = 8.0
MESH = pl.DeviceIdType.MESH
F32 = jnp.float32
BF16 = jnp.bfloat16
NT = (((1,), (1,)), ((), ()))


def tile_of(n, most=256):
    return most if n % most == 0 else n


def ring_place(g, groups):
    half = groups // 2
    return jnp.where(g < half, g, 3 * half - 1 - g)


def gather_kernel(
    groups, inner, first_round, last_round, *refs,
):
    refs = list(refs)
    e_ref, fine_ref, coarse_ref = refs[:3]
    del refs[:3]
    if not first_round:
        moment_in, mass_in = refs[:2]
        del refs[:2]
    moment_ref, mass_ref = refs[:2]
    del refs[:2]
    if last_round:
        coarse_out = refs.pop(0)
    (rows, prob, moment, half_sq, mass, peak, stat,
     up_send, down_send, z_recv, ring_send, ring_recv, sib_send, sib_recv, stat_send, stat_recv, out_sem) = refs[:17]
    layers = inner // 2
    reach = groups // 2
    count = e_ref.shape[0]
    both = 2 * count
    part = count // 2
    width = e_ref.shape[1]
    kl = fine_ref.shape[0]
    kt = tile_of(kl)
    nt = tile_of(width, 512)
    st = tile_of(kl, 512)
    g = lax.axis_index("grp")
    i = lax.axis_index("inner")
    z = i // 2
    core = i % 2
    place = ring_place(g, groups)
    ahead = ring_place((place + 1) % groups, groups)
    behind = ring_place((place + groups - 1) % groups, groups)
    sibling = (g, 2 * z + 1 - core)

    barrier = pltpu.get_barrier_semaphore()
    for off in range(1, inner):
        pl.semaphore_signal(barrier, inc=1, device_id=(g, (i + off) % inner), device_id_type=MESH)
    for off in range(1, groups):
        pl.semaphore_signal(barrier, inc=1, device_id=((g + off) % groups, i), device_id_type=MESH)
    pl.semaphore_wait(barrier, inner + groups - 2)

    low = jnp.minimum(z, layers - 1 - z)
    side = jnp.where(2 * z < layers - 1, 1, -1)

    def layer_at(q):
        near = z + ((q + 1) // 2) * (1 - 2 * (q % 2))
        return jnp.where(q <= 2 * low, near, z + side * (q - low))

    def slots_of(h):
        if h == 0:
            return (0,)
        if h == reach:
            return (groups - 1,)
        return (2 * h - 1, 2 * h)

    def scored_at(h):
        return (0, *slots_of(h)) if h == 1 else slots_of(h)

    def up_copy(zz):
        block = rows.at[zz, 0, core]
        return pltpu.make_async_remote_copy(
            block, block, up_send.at[zz], z_recv.at[zz], (g, i + 2), device_id_type=MESH)

    def down_copy(zz):
        block = rows.at[zz, 0, core]
        return pltpu.make_async_remote_copy(
            block, block, down_send.at[zz], z_recv.at[zz], (g, i - 2), device_id_type=MESH)

    def ring_copy(zz, hop, way):
        source = 0 if hop == 1 else 2 * (hop - 1) - 1 + way
        if hop < reach:
            src, dst = rows.at[zz, source, core], rows.at[zz, 2 * hop - 1 + way, core]
        else:
            piece = pl.ds(way * part, part)
            src, dst = rows.at[zz, source, core, piece], rows.at[zz, groups - 1, core, piece]
        return pltpu.make_async_remote_copy(
            src, dst, ring_send.at[way, zz, hop - 1], ring_recv.at[way, zz, hop - 1],
            (ahead if way == 0 else behind, i), device_id_type=MESH)

    def sib_copy(zz, slot):
        block = rows.at[zz, slot, core]
        return pltpu.make_async_remote_copy(
            block, block, sib_send.at[zz, slot], sib_recv.at[zz, slot], sibling, device_id_type=MESH)

    def sib_arrival(zz, slot):
        block = rows.at[zz, slot, 1 - core]
        return pltpu.make_async_remote_copy(
            block, block, sib_send.at[zz, slot], sib_recv.at[zz, slot], sibling, device_id_type=MESH)

    def goes_up(zz):
        return jnp.logical_and(zz <= z, z < layers - 1)

    def goes_down(zz):
        return jnp.logical_and(zz >= z, z > 0)

    def forward(h, q):
        zz = layer_at(q)
        if h == 0:
            @pl.when(q > 0)
            def _():
                up_copy(zz).wait_recv()

            @pl.when(goes_up(zz))
            def _():
                up_copy(zz).start()

            @pl.when(goes_down(zz))
            def _():
                down_copy(zz).start()
        else:
            for way in (0, 1):
                ring_copy(zz, h, way).wait_recv()
        if h < reach:
            for way in (0, 1):
                ring_copy(zz, h + 1, way).start()
        for slot in slots_of(h):
            sib_copy(zz, slot).start()

    def stat_copy(zz, h, peer):
        slots = scored_at(h)
        piece = stat.at[zz, i, pl.ds(slots[0], len(slots))]
        return pltpu.make_async_remote_copy(
            piece, piece, stat_send.at[zz, h], stat_recv.at[zz, h], (g, peer), device_id_type=MESH)

    def stat_all(zz, h):
        slots = scored_at(h)
        piece = stat.at[zz, pl.ds(0, inner - 1), pl.ds(slots[0], len(slots))]
        return pltpu.make_async_remote_copy(
            piece, piece, stat_send.at[zz, h], stat_recv.at[zz, h], (g, (i + 1) % inner), device_id_type=MESH)

    def score(h, q):
        zz = layer_at(q)
        slots = scored_at(h)
        for slot in slots:
            sib_arrival(zz, slot).wait_recv()
        block = rows[zz, slots[0]:slots[-1] + 1].reshape(len(slots) * both, width)
        tops, totals = [], []
        for t in range(kl // st):
            ks = pl.ds(t * st, st)
            s = lax.dot_general(fine_ref[ks, :], block, NT, preferred_element_type=F32)
            s = s * (1.0 / temper) - jnp.concatenate([half_sq[ks, :]] * len(slots), axis=1)
            top = jnp.max(s, axis=0, keepdims=True)
            e = jnp.exp(s - top)
            for n, slot in enumerate(slots):
                prob[zz, slot, ks, :] = e[:, n * both:(n + 1) * both].astype(BF16)
                peak[zz, slot, t] = top[:, n * both:(n + 1) * both]
            tops.append(top)
            totals.append(jnp.sum(e, axis=0, keepdims=True))
        most = functools.reduce(jnp.maximum, tops)
        total = sum(a * jnp.exp(top - most) for a, top in zip(totals, tops))
        lse = most + jnp.log(total)
        for n, slot in enumerate(slots):
            stat[zz, i, slot] = lse[:, n * both:(n + 1) * both]
        for off in range(1, inner):
            stat_copy(zz, h, (i + off) % inner).start()

    def moments(h, u):
        items = []
        for zz in (layers // 2 - 1 - u, layers // 2 + u):
            stat_all(zz, h).wait_recv()
            for slot in scored_at(h):
                lse = stat[zz, :, slot]
                most = jnp.max(lse, axis=0)
                lse = most + jnp.log(jnp.sum(jnp.exp(lse - most[None]), axis=0))
                items.append((zz, slot, lse))

        for t in range(kl // st):
            ks = pl.ds(t * st, st)
            seen = mass[ks, :]
            parts = []
            for zz, slot, lse in items:
                resp = prob[zz, slot, ks, :].astype(F32) * jnp.exp(peak[zz, slot, t] - lse)
                seen = seen + resp
                parts.append(resp.astype(BF16))
            mass[ks, :] = seen
            left = jnp.concatenate(parts, axis=1)
            for d in range(0, width, nt):
                ds = pl.ds(d, nt)
                right = jnp.concatenate(
                    [rows[zz, slot, :, :, ds].reshape(both, nt) for zz, slot, _ in items], axis=0)
                moment[ks, ds] += jnp.dot(left, right, preferred_element_type=F32)

    rows[z, 0, core] = e_ref[...]
    forward(0, 0)

    def squares(t, carry):
        ks = pl.ds(pl.multiple_of(t * kt, kt), kt)
        f = fine_ref[ks, :].astype(F32)
        half_sq[ks, :] = jnp.broadcast_to(
            (0.5 / temper) * jnp.sum(f * f, axis=1, keepdims=True), (kt, both))
        mass[ks, :] = jnp.zeros((kt, both), F32)
        if not first_round:
            moment[ks, :] = moment_in[ks, :]
        return carry

    lax.fori_loop(0, kl // kt, squares, 0)
    if first_round:
        c = coarse_ref[...].astype(F32)
        c_sq = jnp.broadcast_to(jnp.sum(c * c, axis=1, keepdims=True), (c.shape[0], 128))
        c_half = (0.5 / temper) * jnp.transpose(c_sq)[0:1, :]

        def prior(t, carry):
            ks = pl.ds(pl.multiple_of(t * kt, kt), kt)
            logits = lax.dot_general(fine_ref[ks, :], coarse_ref[...], NT, preferred_element_type=F32)
            logits = logits * (1.0 / temper) - c_half
            e = jnp.exp(logits - jnp.max(logits, axis=1, keepdims=True))
            parent = (e / jnp.sum(e, axis=1, keepdims=True)).astype(BF16)
            moment[ks, :] = shrink * jnp.dot(parent, coarse_ref[...], preferred_element_type=F32)
            return carry

        lax.fori_loop(0, kl // kt, prior, 0)

    def turn(t, carry):
        def gated(h, work):
            q = t - h

            @pl.when(jnp.logical_and(q >= 0, q < layers))
            def _():
                work(h, q)

        def forward_later(h, q):
            @pl.when(t > 0)
            def _():
                forward(h, q)

        for h in (0, 1):
            gated(h, forward_later)
        gated(1, score)
        for h in range(1, reach + 1):
            u = t - h - 1 - layers // 2

            @pl.when(jnp.logical_and(u >= 0, u < layers // 2))
            def _():
                moments(h, u)

        for h in range(2, reach + 1):
            gated(h, forward)
            gated(h, score)
        return carry

    lax.fori_loop(0, layers + reach + 1, turn, 0)

    heavy = jnp.broadcast_to(jnp.sum(mass[...], axis=1, keepdims=True), mass_ref.shape)
    if not first_round:
        heavy = heavy + mass_in[...]
    mass_ref[...] = heavy
    written = pltpu.make_async_copy(moment, moment_ref, out_sem.at[0])
    written.start()
    if last_round:
        finish(groups, inner, coarse_ref, moment, mass_ref, coarse_out, *refs[17:])

    def drain(zz, carry):
        @pl.when(goes_up(zz))
        def _():
            up_copy(zz).wait_send()

        @pl.when(goes_down(zz))
        def _():
            down_copy(zz).wait_send()

        for h in range(reach + 1):
            if h < reach:
                for way in (0, 1):
                    ring_copy(zz, h + 1, way).wait_send()
            for slot in slots_of(h):
                sib_copy(zz, slot).wait_send()
            if h > 0:
                stat_all(zz, h).wait_send()
        return carry

    lax.fori_loop(0, layers, drain, 0)
    written.wait()


def shares_of(groups, inner, coarse_rows):
    piece = 16
    owners = min(inner // 2, coarse_rows // (groups * 2 * piece))
    return piece, owners


def finish(
    groups, inner, coarse_ref, moment_ref, mass_ref, coarse_out,
    fine_low, share, out1, in1, out2, in2, res,
    sem1, send2, recv2, send3, recv3, send4, recv4, send5, recv5,
):
    layers = inner // 2
    kl, width = moment_ref.shape
    coarse_rows = coarse_ref.shape[0]
    piece, owners = shares_of(groups, inner, coarse_rows)
    own_rows = 2 * owners * piece
    kt = tile_of(kl, 512)
    g = lax.axis_index("grp")
    i = lax.axis_index("inner")
    z = i // 2
    core = i % 2
    sibling = (g, 2 * z + 1 - core)

    c = coarse_ref[...].astype(F32)
    c_half = (0.5 / temper) * jnp.sum(c * c, axis=1, keepdims=True)

    def child(t, carry):
        ks = pl.ds(pl.multiple_of(t * kt, kt), kt)
        weight = mass_ref[ks, :] + shrink
        low = (moment_ref[ks, :] * (1.0 / weight[:, 0:1])).astype(BF16)
        fine_low[ks, :] = low
        logits = lax.dot_general(coarse_ref[...], low, NT, preferred_element_type=F32)
        logits = logits * (1.0 / temper) - c_half
        e = jnp.exp(logits - jnp.max(logits, axis=0, keepdims=True))
        scale = jnp.transpose(weight)[0:1, :] / jnp.sum(e, axis=0, keepdims=True)
        share[:, ks] = (e * scale).astype(BF16)
        return carry

    lax.fori_loop(0, kl // kt, child, 0)

    mine = share[pl.ds(pl.multiple_of(g * own_rows, own_rows), own_rows), :]
    numerator = jnp.dot(mine, fine_low[...], preferred_element_type=F32)
    den = jnp.broadcast_to(jnp.sum(mine.astype(F32), axis=1, keepdims=True), (own_rows, 128))

    def packed(total):
        high = total.astype(BF16)
        rest = (total - high.astype(F32)).astype(BF16)
        lane = lax.broadcasted_iota(jnp.int32, total.shape, total.ndim - 1)
        return jnp.where(lane < 64, high.astype(F32), rest.astype(F32)).astype(BF16)

    def unpacked(pair):
        return pair[..., 0:1] + pair[..., 64:65]

    shape = (2, owners, piece)
    out1[:, :, :, :width] = numerator.astype(BF16).reshape(*shape, width)
    out1[:, :, :, width:] = packed(den).reshape(*shape, 128)
    swap = pltpu.make_async_remote_copy(
        out1.at[1 - core], in1, sem1.at[0], sem1.at[1], sibling, device_id_type=MESH)
    swap.start()
    swap.wait_recv()
    a, b = out1[core].astype(F32), in1[...].astype(F32)
    out2[:, :, :width] = (a[..., :width] + b[..., :width]).astype(BF16)
    both_den = jnp.broadcast_to(unpacked(a[..., width:]) + unpacked(b[..., width:]), (owners, piece, 128))
    out2[:, :, width:] = packed(both_den)

    def part_copy(zo):
        return pltpu.make_async_remote_copy(
            out2.at[zo], in2.at[z], send2.at[zo], recv2.at[z], (g, 2 * zo + core), device_id_type=MESH)

    def part_arrival(zs):
        return pltpu.make_async_remote_copy(
            out2.at[0], in2.at[zs], send2.at[0], recv2.at[zs], (g, 2 * zs + core), device_id_type=MESH)

    def done_copy(zt):
        block = res.at[g, core, z]
        return pltpu.make_async_remote_copy(
            block, block, send3.at[zt], recv3.at[z], (g, 2 * zt + core), device_id_type=MESH)

    def done_arrival(zs):
        block = res.at[g, core, zs]
        return pltpu.make_async_remote_copy(
            block, block, send3.at[zs], recv3.at[zs], (g, 2 * zs + core), device_id_type=MESH)

    def when_owner(zo, work):
        if owners == layers:
            work()
        else:
            pl.when(zo < owners)(work)

    for off in range(1, layers):
        zo = (z + off) % layers
        when_owner(zo, lambda zo=zo: part_copy(zo).start())

    def own():
        for off in range(1, layers):
            part_arrival((z + off) % layers).wait_recv()
        in2[z] = out2[z]
        got = in2[...].astype(F32)
        num = jnp.sum(got[..., :width], axis=0)
        total = jnp.sum(unpacked(got[..., width:]), axis=0)
        at = pl.multiple_of(g * own_rows + (core * owners + z) * piece, piece)
        old = coarse_ref[pl.ds(at, piece), :].astype(F32)
        res[g, core, z] = ((num + anchor * old) / (total + anchor)).astype(BF16)
        for off in range(1, layers):
            done_copy((z + off) % layers).start()

    when_owner(z, own)
    for off in range(1, layers):
        zo = (z + off) % layers
        when_owner(zo, lambda zo=zo: done_arrival(zo).wait_recv())

    def group_copy(gt):
        block = res.at[g, core]
        return pltpu.make_async_remote_copy(
            block, block, send4.at[gt], recv4.at[g], (gt, i), device_id_type=MESH)

    def group_arrival(gs):
        block = res.at[gs, core]
        return pltpu.make_async_remote_copy(
            block, block, send4.at[gs], recv4.at[gs], (gs, i), device_id_type=MESH)

    def over(gs):
        block = res.at[gs, core]
        return pltpu.make_async_remote_copy(
            block, block, send5.at[gs], recv5.at[gs], sibling, device_id_type=MESH)

    def over_arrival(gs):
        block = res.at[gs, 1 - core]
        return pltpu.make_async_remote_copy(
            block, block, send5.at[gs], recv5.at[gs], sibling, device_id_type=MESH)

    for off in range(1, groups):
        group_copy((g + off) % groups).start()
    over(g).start()
    for off in range(1, groups):
        gs = (g + off) % groups
        group_arrival(gs).wait_recv()
        over(gs).start()
    for gs in range(groups):
        over_arrival(gs).wait_recv()
    coarse_out[...] = res[...].reshape(coarse_rows, width)

    swap.wait_send()
    for off in range(1, layers):
        zo = (z + off) % layers
        when_owner(zo, lambda zo=zo: part_copy(zo).wait_send())
        when_owner(z, lambda zo=zo: done_copy(zo).wait_send())
    for off in range(1, groups):
        group_copy((g + off) % groups).wait_send()
    for gs in range(groups):
        over(gs).wait_send()


def gathered_moments(groups, inner, number, rounds, embeds, fine, coarse, before):
    layers, reach = inner // 2, groups // 2
    count, width = embeds.shape
    kl = fine.shape[0]
    coarse_rows = coarse.shape[0]
    both = 2 * count
    dma = pltpu.SemaphoreType.DMA
    vm = pl.BlockSpec(memory_space=pltpu.VMEM)
    total = groups * inner * count
    last = number == rounds - 1
    out_shape = [jax.ShapeDtypeStruct((kl, width), F32), jax.ShapeDtypeStruct((kl, 128), F32)]
    scratch = [
        pltpu.VMEM((layers, groups, 2, count, width), BF16),
        pltpu.VMEM((layers, groups, kl, both), BF16),
        pltpu.VMEM((kl, width), F32),
        pltpu.VMEM((kl, both), F32),
        pltpu.VMEM((kl, both), F32),
        pltpu.VMEM((layers, groups, kl // tile_of(kl, 512), 1, both), F32),
        pltpu.VMEM((layers, inner, groups, 1, both), F32),
        dma((layers,)), dma((layers,)), dma((layers,)),
        dma((2, layers, reach)), dma((2, layers, reach)),
        dma((layers, groups)), dma((layers, groups)),
        dma((layers, reach + 1)), dma((layers, reach + 1)), dma((1,)),
    ]
    if last:
        piece, owners = shares_of(groups, inner, coarse_rows)
        wide = width + 128
        out_shape.append(jax.ShapeDtypeStruct((coarse_rows, width), BF16))
        scratch += [
            pltpu.VMEM((kl, width), BF16),
            pltpu.VMEM((coarse_rows, kl), BF16),
            pltpu.VMEM((2, owners, piece, wide), BF16),
            pltpu.VMEM((owners, piece, wide), BF16),
            pltpu.VMEM((owners, piece, wide), BF16),
            pltpu.VMEM((layers, piece, wide), BF16),
            pltpu.VMEM((groups, 2, owners, piece, width), BF16),
            dma((2,)), dma((layers,)), dma((layers,)), dma((layers,)), dma((layers,)),
            dma((groups,)), dma((groups,)), dma((groups,)), dma((groups,)),
        ]
    args = (embeds, fine, coarse, *before)
    return pl.pallas_call(
        functools.partial(gather_kernel, groups, inner, number == 0, last),
        out_shape=out_shape,
        in_specs=[vm] * len(args),
        out_specs=[pl.BlockSpec(memory_space=pl.ANY)] + [vm] * (len(out_shape) - 1),
        scratch_shapes=scratch,
        compiler_params=pltpu.CompilerParams(
            collective_id=number, has_side_effects=True, vmem_limit_bytes=60 * 1024 * 1024),
        cost_estimate=pl.CostEstimate(
            flops=4 * total * kl * width, bytes_accessed=8 * kl * width, transcendentals=total * kl),
    )(*args)


def output_kernel(moment_ref, mass_ref, coarse_ref, fine_out, coarse_out):
    fine_out[...] = moment_ref[...] * (1.0 / (mass_ref[:, 0:1] + shrink))
    coarse_out[...] = coarse_ref[...].astype(F32)


def outputs(moment, mass, coarse):
    steps = 8
    kl, width = moment.shape
    coarse_rows = coarse.shape[0]

    def block(count, columns):
        return pl.BlockSpec((count // steps, columns), lambda t: (t, 0))

    return pl.pallas_call(
        output_kernel,
        grid=(steps,),
        out_shape=[jax.ShapeDtypeStruct((kl, width), F32), jax.ShapeDtypeStruct((coarse_rows, width), F32)],
        in_specs=[block(kl, width), block(kl, mass.shape[1]), block(coarse_rows, width)],
        out_specs=[block(kl, width), block(coarse_rows, width)],
    )(moment, mass, coarse)


def on_device(groups, inner, embeds, fine_centroids, coarse_centroids):
    count, width = embeds.shape
    kl = fine_centroids.shape[0]
    rounds = 1
    while groups * inner * (count // rounds) * (width + kl) * 2 > 34 * 1024 * 1024:
        rounds *= 2
    step = count // rounds
    found = ()
    for r in range(rounds):
        found = gathered_moments(
            groups, inner, r, rounds, embeds[r * step:(r + 1) * step], fine_centroids, coarse_centroids, found[:2])
    return tuple(outputs(*found))


def solution(mesh):
    return jax.shard_map(
        functools.partial(on_device, mesh.shape["grp"], mesh.shape["inner"]),
        mesh=mesh,
        in_specs=(P(("grp", "inner"), None), P("inner", None), P()),
        out_specs=(P("inner", None), P()),
        check_vma=False,
    )
```

```python
import functools

import jax
import jax.numpy as jnp
from jax import lax
from jax.experimental import pallas as pl
from jax.experimental.pallas import tpu as pltpu
from jax.sharding import PartitionSpec as P

temper = 0.02
shrink = 1.0
anchor = 8.0
MESH = pl.DeviceIdType.MESH
F32 = jnp.float32
BF16 = jnp.bfloat16
NT = (((1,), (1,)), ((), ()))


def tile_of(n, most=256):
    return most if n % most == 0 else n


def ring_place(g, groups):
    half = groups // 2
    return jnp.where(g < half, g, 3 * half - 1 - g)


def gather_kernel(
    groups, inner, first_round, last_round, *refs,
):
    refs = list(refs)
    e_ref, fine_ref, coarse_ref = refs[:3]
    del refs[:3]
    if not first_round:
        moment_in, mass_in = refs[:2]
        del refs[:2]
    moment_ref, mass_ref = refs[:2]
    del refs[:2]
    if last_round:
        coarse_out = refs.pop(0)
    (rows, prob, moment, half_sq, mass, peak, stat,
     up_send, down_send, z_recv, ring_send, ring_recv, sib_send, sib_recv, stat_send, stat_recv, out_sem) = refs[:17]
    layers = inner // 2
    reach = groups // 2
    count = e_ref.shape[0]
    both = 2 * count
    part = count // 2
    width = e_ref.shape[1]
    kl = fine_ref.shape[0]
    kt = tile_of(kl)
    nt = tile_of(width, 512)
    st = tile_of(kl, 512)
    g = lax.axis_index("grp")
    i = lax.axis_index("inner")
    z = i // 2
    core = i % 2
    place = ring_place(g, groups)
    ahead = ring_place((place + 1) % groups, groups)
    behind = ring_place((place + groups - 1) % groups, groups)
    sibling = (g, 2 * z + 1 - core)

    barrier = pltpu.get_barrier_semaphore()
    for off in range(1, inner):
        pl.semaphore_signal(barrier, inc=1, device_id=(g, (i + off) % inner), device_id_type=MESH)
    for off in range(1, groups):
        pl.semaphore_signal(barrier, inc=1, device_id=((g + off) % groups, i), device_id_type=MESH)
    pl.semaphore_wait(barrier, inner + groups - 2)

    low = jnp.minimum(z, layers - 1 - z)
    side = jnp.where(2 * z < layers - 1, 1, -1)

    def layer_at(q):
        near = z + ((q + 1) // 2) * (1 - 2 * (q % 2))
        return jnp.where(q <= 2 * low, near, z + side * (q - low))

    def slots_of(h):
        if h == 0:
            return (0,)
        if h == reach:
            return (groups - 1,)
        return (2 * h - 1, 2 * h)

    def scored_at(h):
        return (0, *slots_of(h)) if h == 1 else slots_of(h)

    def up_copy(zz):
        block = rows.at[zz, 0, core]
        return pltpu.make_async_remote_copy(
            block, block, up_send.at[zz], z_recv.at[zz], (g, i + 2), device_id_type=MESH)

    def down_copy(zz):
        block = rows.at[zz, 0, core]
        return pltpu.make_async_remote_copy(
            block, block, down_send.at[zz], z_recv.at[zz], (g, i - 2), device_id_type=MESH)

    def ring_copy(zz, hop, way):
        source = 0 if hop == 1 else 2 * (hop - 1) - 1 + way
        if hop < reach:
            src, dst = rows.at[zz, source, core], rows.at[zz, 2 * hop - 1 + way, core]
        else:
            piece = pl.ds(way * part, part)
            src, dst = rows.at[zz, source, core, piece], rows.at[zz, groups - 1, core, piece]
        return pltpu.make_async_remote_copy(
            src, dst, ring_send.at[way, zz, hop - 1], ring_recv.at[way, zz, hop - 1],
            (ahead if way == 0 else behind, i), device_id_type=MESH)

    def sib_copy(zz, slot):
        block = rows.at[zz, slot, core]
        return pltpu.make_async_remote_copy(
            block, block, sib_send.at[zz, slot], sib_recv.at[zz, slot], sibling, device_id_type=MESH)

    def sib_arrival(zz, slot):
        block = rows.at[zz, slot, 1 - core]
        return pltpu.make_async_remote_copy(
            block, block, sib_send.at[zz, slot], sib_recv.at[zz, slot], sibling, device_id_type=MESH)

    def goes_up(zz):
        return jnp.logical_and(zz <= z, z < layers - 1)

    def goes_down(zz):
        return jnp.logical_and(zz >= z, z > 0)

    def forward(h, q):
        zz = layer_at(q)
        if h == 0:
            @pl.when(q > 0)
            def _():
                up_copy(zz).wait_recv()

            @pl.when(goes_up(zz))
            def _():
                up_copy(zz).start()

            @pl.when(goes_down(zz))
            def _():
                down_copy(zz).start()
        else:
            for way in (0, 1):
                ring_copy(zz, h, way).wait_recv()
        if h < reach:
            for way in (0, 1):
                ring_copy(zz, h + 1, way).start()
        for slot in slots_of(h):
            sib_copy(zz, slot).start()

    def stat_copy(zz, h, peer):
        slots = scored_at(h)
        piece = stat.at[zz, i, pl.ds(slots[0], len(slots))]
        return pltpu.make_async_remote_copy(
            piece, piece, stat_send.at[zz, h], stat_recv.at[zz, h], (g, peer), device_id_type=MESH)

    def stat_all(zz, h):
        slots = scored_at(h)
        piece = stat.at[zz, pl.ds(0, inner - 1), pl.ds(slots[0], len(slots))]
        return pltpu.make_async_remote_copy(
            piece, piece, stat_send.at[zz, h], stat_recv.at[zz, h], (g, (i + 1) % inner), device_id_type=MESH)

    def score(h, q):
        zz = layer_at(q)
        slots = scored_at(h)
        for slot in slots:
            sib_arrival(zz, slot).wait_recv()
        block = rows[zz, slots[0]:slots[-1] + 1].reshape(len(slots) * both, width)
        tops, totals = [], []
        for t in range(kl // st):
            ks = pl.ds(t * st, st)
            s = lax.dot_general(fine_ref[ks, :], block, NT, preferred_element_type=F32)
            s = s * (1.0 / temper) - jnp.concatenate([half_sq[ks, :]] * len(slots), axis=1)
            top = jnp.max(s, axis=0, keepdims=True)
            e = jnp.exp(s - top)
            for n, slot in enumerate(slots):
                prob[zz, slot, ks, :] = e[:, n * both:(n + 1) * both].astype(BF16)
                peak[zz, slot, t] = top[:, n * both:(n + 1) * both]
            tops.append(top)
            totals.append(jnp.sum(e, axis=0, keepdims=True))
        most = functools.reduce(jnp.maximum, tops)
        total = sum(a * jnp.exp(top - most) for a, top in zip(totals, tops))
        lse = most + jnp.log(total)
        for n, slot in enumerate(slots):
            stat[zz, i, slot] = lse[:, n * both:(n + 1) * both]
        for off in range(1, inner):
            stat_copy(zz, h, (i + off) % inner).start()

    def moments(h, u):
        items = []
        for zz in (layers // 2 - 1 - u, layers // 2 + u):
            stat_all(zz, h).wait_recv()
            for slot in scored_at(h):
                lse = stat[zz, :, slot]
                most = jnp.max(lse, axis=0)
                lse = most + jnp.log(jnp.sum(jnp.exp(lse - most[None]), axis=0))
                items.append((zz, slot, lse))

        for t in range(kl // st):
            ks = pl.ds(t * st, st)
            seen = mass[ks, :]
            parts = []
            for zz, slot, lse in items:
                resp = prob[zz, slot, ks, :].astype(F32) * jnp.exp(peak[zz, slot, t] - lse)
                seen = seen + resp
                parts.append(resp.astype(BF16))
            mass[ks, :] = seen
            left = jnp.concatenate(parts, axis=1)
            for d in range(0, width, nt):
                ds = pl.ds(d, nt)
                right = jnp.concatenate(
                    [rows[zz, slot, :, :, ds].reshape(both, nt) for zz, slot, _ in items], axis=0)
                moment[ks, ds] += jnp.dot(left, right, preferred_element_type=F32)

    rows[z, 0, core] = e_ref[...]
    forward(0, 0)

    def squares(t, carry):
        ks = pl.ds(pl.multiple_of(t * kt, kt), kt)
        f = fine_ref[ks, :].astype(F32)
        half_sq[ks, :] = jnp.broadcast_to(
            (0.5 / temper) * jnp.sum(f * f, axis=1, keepdims=True), (kt, both))
        mass[ks, :] = jnp.zeros((kt, both), F32)
        if not first_round:
            moment[ks, :] = moment_in[ks, :]
        return carry

    lax.fori_loop(0, kl // kt, squares, 0)
    if first_round:
        c = coarse_ref[...].astype(F32)
        c_sq = jnp.broadcast_to(jnp.sum(c * c, axis=1, keepdims=True), (c.shape[0], 128))
        c_half = (0.5 / temper) * jnp.transpose(c_sq)[0:1, :]

        def prior(t, carry):
            ks = pl.ds(pl.multiple_of(t * kt, kt), kt)
            logits = lax.dot_general(fine_ref[ks, :], coarse_ref[...], NT, preferred_element_type=F32)
            logits = logits * (1.0 / temper) - c_half
            e = jnp.exp(logits - jnp.max(logits, axis=1, keepdims=True))
            parent = (e / jnp.sum(e, axis=1, keepdims=True)).astype(BF16)
            moment[ks, :] = shrink * jnp.dot(parent, coarse_ref[...], preferred_element_type=F32)
            return carry

        lax.fori_loop(0, kl // kt, prior, 0)

    def turn(t, carry):
        def gated(h, work):
            q = t - h

            @pl.when(jnp.logical_and(q >= 0, q < layers))
            def _():
                work(h, q)

        def forward_later(h, q):
            @pl.when(t > 0)
            def _():
                forward(h, q)

        for h in (0, 1):
            gated(h, forward_later)
        gated(1, score)
        for h in range(1, reach + 1):
            u = t - h - 1 - layers // 2

            @pl.when(jnp.logical_and(u >= 0, u < layers // 2))
            def _():
                moments(h, u)

        for h in range(2, reach + 1):
            gated(h, forward)
            gated(h, score)
        return carry

    lax.fori_loop(0, layers + reach + 1, turn, 0)

    heavy = jnp.broadcast_to(jnp.sum(mass[...], axis=1, keepdims=True), mass_ref.shape)
    if not first_round:
        heavy = heavy + mass_in[...]
    mass_ref[...] = heavy
    written = pltpu.make_async_copy(moment, moment_ref, out_sem.at[0])
    written.start()
    if last_round:
        finish(groups, inner, coarse_ref, moment, mass_ref, coarse_out, *refs[17:])

    def drain(zz, carry):
        @pl.when(goes_up(zz))
        def _():
            up_copy(zz).wait_send()

        @pl.when(goes_down(zz))
        def _():
            down_copy(zz).wait_send()

        for h in range(reach + 1):
            if h < reach:
                for way in (0, 1):
                    ring_copy(zz, h + 1, way).wait_send()
            for slot in slots_of(h):
                sib_copy(zz, slot).wait_send()
            if h > 0:
                stat_all(zz, h).wait_send()
        return carry

    lax.fori_loop(0, layers, drain, 0)
    written.wait()


def shares_of(groups, inner, coarse_rows):
    piece = 16
    owners = min(inner // 2, coarse_rows // (groups * 2 * piece))
    return piece, owners


def finish(
    groups, inner, coarse_ref, moment_ref, mass_ref, coarse_out,
    fine_low, share, out1, in1, out2, in2, res,
    sem1, send2, recv2, send3, recv3, send4, recv4, send5, recv5,
):
    layers = inner // 2
    kl, width = moment_ref.shape
    coarse_rows = coarse_ref.shape[0]
    piece, owners = shares_of(groups, inner, coarse_rows)
    own_rows = 2 * owners * piece
    kt = tile_of(kl, 512)
    g = lax.axis_index("grp")
    i = lax.axis_index("inner")
    z = i // 2
    core = i % 2
    sibling = (g, 2 * z + 1 - core)

    c = coarse_ref[...].astype(F32)
    c_half = (0.5 / temper) * jnp.sum(c * c, axis=1, keepdims=True)

    def child(t, carry):
        ks = pl.ds(pl.multiple_of(t * kt, kt), kt)
        weight = mass_ref[ks, :] + shrink
        low = (moment_ref[ks, :] * (1.0 / weight[:, 0:1])).astype(BF16)
        fine_low[ks, :] = low
        logits = lax.dot_general(coarse_ref[...], low, NT, preferred_element_type=F32)
        logits = logits * (1.0 / temper) - c_half
        e = jnp.exp(logits - jnp.max(logits, axis=0, keepdims=True))
        scale = jnp.transpose(weight)[0:1, :] / jnp.sum(e, axis=0, keepdims=True)
        share[:, ks] = (e * scale).astype(BF16)
        return carry

    lax.fori_loop(0, kl // kt, child, 0)

    mine = share[pl.ds(pl.multiple_of(g * own_rows, own_rows), own_rows), :]
    numerator = jnp.dot(mine, fine_low[...], preferred_element_type=F32)
    den = jnp.broadcast_to(jnp.sum(mine.astype(F32), axis=1, keepdims=True), (own_rows, 128))

    def packed(total):
        high = total.astype(BF16)
        rest = (total - high.astype(F32)).astype(BF16)
        lane = lax.broadcasted_iota(jnp.int32, total.shape, total.ndim - 1)
        return jnp.where(lane < 64, high.astype(F32), rest.astype(F32)).astype(BF16)

    def unpacked(pair):
        return pair[..., 0:1] + pair[..., 64:65]

    shape = (2, owners, piece)
    out1[:, :, :, :width] = numerator.astype(BF16).reshape(*shape, width)
    out1[:, :, :, width:] = packed(den).reshape(*shape, 128)
    swap = pltpu.make_async_remote_copy(
        out1.at[1 - core], in1, sem1.at[0], sem1.at[1], sibling, device_id_type=MESH)
    swap.start()
    swap.wait_recv()
    a, b = out1[core].astype(F32), in1[...].astype(F32)
    out2[:, :, :width] = (a[..., :width] + b[..., :width]).astype(BF16)
    both_den = jnp.broadcast_to(unpacked(a[..., width:]) + unpacked(b[..., width:]), (owners, piece, 128))
    out2[:, :, width:] = packed(both_den)

    def part_copy(zo):
        return pltpu.make_async_remote_copy(
            out2.at[zo], in2.at[z], send2.at[zo], recv2.at[z], (g, 2 * zo + core), device_id_type=MESH)

    def part_arrival(zs):
        return pltpu.make_async_remote_copy(
            out2.at[0], in2.at[zs], send2.at[0], recv2.at[zs], (g, 2 * zs + core), device_id_type=MESH)

    def done_copy(zt):
        block = res.at[g, core, z]
        return pltpu.make_async_remote_copy(
            block, block, send3.at[zt], recv3.at[z], (g, 2 * zt + core), device_id_type=MESH)

    def done_arrival(zs):
        block = res.at[g, core, zs]
        return pltpu.make_async_remote_copy(
            block, block, send3.at[zs], recv3.at[zs], (g, 2 * zs + core), device_id_type=MESH)

    def when_owner(zo, work):
        if owners == layers:
            work()
        else:
            pl.when(zo < owners)(work)

    for off in range(1, layers):
        zo = (z + off) % layers
        when_owner(zo, lambda zo=zo: part_copy(zo).start())

    def own():
        for off in range(1, layers):
            part_arrival((z + off) % layers).wait_recv()
        in2[z] = out2[z]
        got = in2[...].astype(F32)
        num = jnp.sum(got[..., :width], axis=0)
        total = jnp.sum(unpacked(got[..., width:]), axis=0)
        at = pl.multiple_of(g * own_rows + (core * owners + z) * piece, piece)
        old = coarse_ref[pl.ds(at, piece), :].astype(F32)
        res[g, core, z] = ((num + anchor * old) / (total + anchor)).astype(BF16)
        for off in range(1, layers):
            done_copy((z + off) % layers).start()

    when_owner(z, own)
    for off in range(1, layers):
        zo = (z + off) % layers
        when_owner(zo, lambda zo=zo: done_arrival(zo).wait_recv())

    def group_copy(gt):
        block = res.at[g, core]
        return pltpu.make_async_remote_copy(
            block, block, send4.at[gt], recv4.at[g], (gt, i), device_id_type=MESH)

    def group_arrival(gs):
        block = res.at[gs, core]
        return pltpu.make_async_remote_copy(
            block, block, send4.at[gs], recv4.at[gs], (gs, i), device_id_type=MESH)

    def over(gs):
        block = res.at[gs, core]
        return pltpu.make_async_remote_copy(
            block, block, send5.at[gs], recv5.at[gs], sibling, device_id_type=MESH)

    def over_arrival(gs):
        block = res.at[gs, 1 - core]
        return pltpu.make_async_remote_copy(
            block, block, send5.at[gs], recv5.at[gs], sibling, device_id_type=MESH)

    for off in range(1, groups):
        group_copy((g + off) % groups).start()
    over(g).start()
    for off in range(1, groups):
        gs = (g + off) % groups
        group_arrival(gs).wait_recv()
        over(gs).start()
    for gs in range(groups):
        over_arrival(gs).wait_recv()
    coarse_out[...] = res[...].reshape(coarse_rows, width)

    swap.wait_send()
    for off in range(1, layers):
        zo = (z + off) % layers
        when_owner(zo, lambda zo=zo: part_copy(zo).wait_send())
        when_owner(z, lambda zo=zo: done_copy(zo).wait_send())
    for off in range(1, groups):
        group_copy((g + off) % groups).wait_send()
    for gs in range(groups):
        over(gs).wait_send()


def gathered_moments(groups, inner, number, rounds, embeds, fine, coarse, before):
    layers, reach = inner // 2, groups // 2
    count, width = embeds.shape
    kl = fine.shape[0]
    coarse_rows = coarse.shape[0]
    both = 2 * count
    dma = pltpu.SemaphoreType.DMA
    vm = pl.BlockSpec(memory_space=pltpu.VMEM)
    total = groups * inner * count
    last = number == rounds - 1
    out_shape = [jax.ShapeDtypeStruct((kl, width), F32), jax.ShapeDtypeStruct((kl, 128), F32)]
    scratch = [
        pltpu.VMEM((layers, groups, 2, count, width), BF16),
        pltpu.VMEM((layers, groups, kl, both), BF16),
        pltpu.VMEM((kl, width), F32),
        pltpu.VMEM((kl, both), F32),
        pltpu.VMEM((kl, both), F32),
        pltpu.VMEM((layers, groups, kl // tile_of(kl, 512), 1, both), F32),
        pltpu.VMEM((layers, inner, groups, 1, both), F32),
        dma((layers,)), dma((layers,)), dma((layers,)),
        dma((2, layers, reach)), dma((2, layers, reach)),
        dma((layers, groups)), dma((layers, groups)),
        dma((layers, reach + 1)), dma((layers, reach + 1)), dma((1,)),
    ]
    if last:
        piece, owners = shares_of(groups, inner, coarse_rows)
        wide = width + 128
        out_shape.append(jax.ShapeDtypeStruct((coarse_rows, width), BF16))
        scratch += [
            pltpu.VMEM((kl, width), BF16),
            pltpu.VMEM((coarse_rows, kl), BF16),
            pltpu.VMEM((2, owners, piece, wide), BF16),
            pltpu.VMEM((owners, piece, wide), BF16),
            pltpu.VMEM((owners, piece, wide), BF16),
            pltpu.VMEM((layers, piece, wide), BF16),
            pltpu.VMEM((groups, 2, owners, piece, width), BF16),
            dma((2,)), dma((layers,)), dma((layers,)), dma((layers,)), dma((layers,)),
            dma((groups,)), dma((groups,)), dma((groups,)), dma((groups,)),
        ]
    args = (embeds, fine, coarse, *before)
    return pl.pallas_call(
        functools.partial(gather_kernel, groups, inner, number == 0, last),
        out_shape=out_shape,
        in_specs=[vm] * len(args),
        out_specs=[pl.BlockSpec(memory_space=pl.ANY)] + [vm] * (len(out_shape) - 1),
        scratch_shapes=scratch,
        compiler_params=pltpu.CompilerParams(
            collective_id=number, has_side_effects=True, vmem_limit_bytes=60 * 1024 * 1024),
        cost_estimate=pl.CostEstimate(
            flops=4 * total * kl * width, bytes_accessed=8 * kl * width, transcendentals=total * kl),
    )(*args)


def output_kernel(moment_ref, mass_ref, coarse_ref, fine_out, coarse_out):
    fine_out[...] = moment_ref[...] * (1.0 / (mass_ref[:, 0:1] + shrink))
    coarse_out[...] = coarse_ref[...].astype(F32)


def outputs(moment, mass, coarse):
    steps = 2
    kl, width = moment.shape
    coarse_rows = coarse.shape[0]

    def block(count, columns):
        return pl.BlockSpec((count // steps, columns), lambda t: (t, 0))

    return pl.pallas_call(
        output_kernel,
        grid=(steps,),
        out_shape=[jax.ShapeDtypeStruct((kl, width), F32), jax.ShapeDtypeStruct((coarse_rows, width), F32)],
        in_specs=[block(kl, width), block(kl, mass.shape[1]), block(coarse_rows, width)],
        out_specs=[block(kl, width), block(coarse_rows, width)],
    )(moment, mass, coarse)


def on_device(groups, inner, embeds, fine_centroids, coarse_centroids):
    count, width = embeds.shape
    kl = fine_centroids.shape[0]
    rounds = 1
    while groups * inner * (count // rounds) * (width + kl) * 2 > 34 * 1024 * 1024:
        rounds *= 2
    step = count // rounds
    found = ()
    for r in range(rounds):
        found = gathered_moments(
            groups, inner, r, rounds, embeds[r * step:(r + 1) * step], fine_centroids, coarse_centroids, found[:2])
    return tuple(outputs(*found))


def solution(mesh):
    return jax.shard_map(
        functools.partial(on_device, mesh.shape["grp"], mesh.shape["inner"]),
        mesh=mesh,
        in_specs=(P(("grp", "inner"), None), P("inner", None), P()),
        out_specs=(P("inner", None), P()),
        check_vma=False,
    )
```
